32 devices in a mesh: rep: 2 (over y), gx: 4 (over z), gy: 4 (over x, core).
Axes of the slice: x: 2, y: 2, z: 4, core: 2. Of those that a mesh axis runs over, the one named last changes fastest.
Arguments:
- right_side: float32 [64, 128, 128], P(('rep', 'gx'), 'gy'), parts along dimension 0, may hold values from -240 to 240
- dielectric: bfloat16 [64, 128, 128], P(('rep', 'gx'), 'gy'), parts along dimension 0, may hold values from 2 to 80
- screening: bfloat16 [64, 128, 128], P(('rep', 'gx'), 'gy'), parts along dimension 0, may hold values from 0.049804688 to 8
- weights: bfloat16 [8, 4, 8, 8, 4096], P(('rep', 'gx'), 'gy'), parts along dimension 0, may hold values from -0.375 to 0.375
- charges: float32 [8, 4, 64], P(('rep', 'gx'), 'gy'), parts along dimension 0, may hold values from -1 to 1
- owners: int32 [8, 4, 64, 1], P(('rep', 'gx'), 'gy'), parts along dimension 0, may hold values from 0 to 3; in each aligned block of 64 rows (0 to 63, 64 to 127, ..., all dimensions but the last counted through in order) at most 32 rows name the same one
Outputs:
- potential: float32 [64, 128, 128], P(('rep', 'gx'), 'gy'), parts along dimension 0
- atom_forces: float32 [8, 4, 4, 3, 32], P(('rep', 'gx'), 'gy'), parts along dimension 0
The draws below stay inside these ranges and needn't reach their ends.
There are 2 independent parts, one for each index of `rep`. The reference program is written for one: setup_inputs(seed, part) draws one part's arguments, and reference() takes and returns one part's arrays. A program takes and returns all parts, laid end to end along the dimension named above; each array names one. Nothing has to cross between parts.
Inputs may be any that keep to these rules, and one draw needn't show every extreme that they name: `owners`: the 64 atoms of one pencil name any one owner at most 32 times.
All inputs are finite; a program needn't handle non-finite values.
Results may differ from the reference program's by a relative error of at most 0.0021.
The reference program's roundings to bfloat16 on the way (of `gradient`) count: a program that leaves them out, or rounds other values in their place, can miss the bound.
Values sent between devices are 32-bit elements; how exact they have to be, the bound alone decides.
A program may use at most 64 MiB of HBM per device.

```python
import math
import jax
import jax.numpy as jnp
import numpy as np
from jax import lax

CX = 8
CY = 32
NZ = 128
BZ = 16
SLOTS = 8
PRE_SWEEPS = 2
POST_SWEEPS = 2
COARSE_SWEEPS = 6
NX = 32
NY = 128
NB = 8
BLOCK_CELLS = 4096
ATOM_DEV = 64
CAP = 32
N_GX = 4
N_GY = 4


def draw_right_side(key, part):
    key = jax.random.fold_in(key, 11)
    return jnp.clip(40.0 * jax.random.normal(key, (NX, NY, NZ), jnp.float32), -240.0, 240.0)


def levels(key, extent, pieces, smallest, top_value):
    loudness = 1.0
    for dim, blocks in pieces:
        draws = jax.random.uniform(jax.random.fold_in(jax.random.fold_in(key, 6), dim), (blocks,), jnp.float32, smallest / len(pieces), top_value / len(pieces))
        loudness = loudness * jnp.repeat(jnp.exp(draws), extent[dim] // blocks).reshape((-1,) + (1,) * (len(extent) - 1 - dim))
    return loudness


def routed_block(stream_key, own, number, rows, count, top, most, skew):
    sequence = jax.random.permutation(stream_key, count)
    crowded, common = shares(count, rows * top, most, skew, True), shares(count, rows * top, most, skew, False)
    places = jnp.arange(count)

    def named(tallies, offset_by):
        used = int((tallies > 0).sum())
        fixed = max(1, used // 4)
        passed = fixed + (places - fixed + offset_by * (used - fixed)) % max(1, count - fixed)
        return jnp.zeros((count,), jnp.int32).at[sequence[jnp.where(places < fixed, places, passed)]].set(jnp.asarray(tallies, jnp.int32))

    tallies = jnp.where(number % 4 == 0, named(crowded, number // 4), named(common, number - number // 4 - 1))
    mixed = jax.random.permutation(jax.random.fold_in(own, 3), count)
    source_of, sink = mixed[0:count // 2 * 2:2], mixed[1:count // 2 * 2:2]
    margin = jnp.minimum(tallies[source_of] - 1, most - tallies[sink]) // 2
    margin = jnp.where((source_of == sequence[0]) | (sink == sequence[0]) | (tallies[sink] == 0), 0, jnp.maximum(margin, 0))
    passed = jax.random.randint(jax.random.fold_in(own, 4), (count // 2,), 0, 1 << 20) % (margin + 1)
    tallies = tallies.at[source_of].add(-passed).at[sink].add(passed)
    items = jnp.searchsorted(jnp.cumsum(tallies), jnp.arange(rows * top), side="right").astype(jnp.int32)
    table = items.reshape(top, rows).T
    table = table[jax.random.permutation(jax.random.fold_in(own, 1), rows)]
    offset_by = jax.random.randint(jax.random.fold_in(own, 2), (rows, 1), 0, top)
    return jnp.take_along_axis(table, (jnp.arange(top)[None, :] + offset_by) % top, axis=1)


def shares(number_of, total, reach, lean, full):
    loads = [(1 << 20) // math.isqrt(grade ** lean) + 1 for grade in range(1, number_of + 1)]
    largest = reach if full else min(reach, max(-(-total // number_of), total * loads[0] // sum(loads)))
    least = 1 if total - largest >= number_of - 1 else 0
    holding, rest = [largest] + [least] * (number_of - 1), total - largest - least * (number_of - 1)
    while rest > 0:
        movable = [i for i in range(1, number_of) if holding[i] < largest] or [i for i in range(1, number_of) if holding[i] < reach]
        whole, budget = sum([loads[i] for i in movable]), rest
        for i in movable:
            addition = min(reach - holding[i], max(1, budget * loads[i] // whole), rest)
            holding[i] = holding[i] + addition
            rest = rest - addition
    return np.array(holding)


def scatter_about(key, extent, scale, reach, shards=(), kind=jnp.bfloat16):
    values = jax.random.normal(key, extent, jnp.float32) * scale
    if len(shards) > 0:
        values = levels(key, extent, shards, -0.22, 0.18) * values
    return jnp.clip(values, min=-reach, max=reach).astype(kind)


def setup_inputs(seed: int = 0, part: int = 0) -> dict:
    keys = jax.random.split(jax.random.key(seed), 7)
    own_keys = jax.random.split(jax.random.fold_in(keys[6], part), 7)
    right_side = draw_right_side(jax.random.fold_in(jax.random.fold_in(keys[6], part), 71), part)
    dielectric = jnp.clip(jnp.exp(math.log(80.0) - 3.6888795 * jax.random.uniform(own_keys[1], (NX, NY, NZ), jnp.float32) ** levels(own_keys[1], (NX, NY, NZ), ((0, 4), (1, 4)), -0.2, 0.2)), 2.0, 80.0).astype(jnp.bfloat16)
    screening = jnp.clip(jnp.exp(math.log(8.0) - 5.0790877 * jax.random.uniform(own_keys[2], (NX, NY, NZ), jnp.float32) ** levels(own_keys[2], (NX, NY, NZ), ((0, 4), (1, 4)), -0.2, 0.2)), 0.049804688, 8.0).astype(jnp.bfloat16)
    weights = scatter_about(own_keys[3], (N_GX, N_GY, NB, SLOTS, BLOCK_CELLS), (BLOCK_CELLS // 16) ** -0.5, 0.375, ((0, 4), (1, 4)))
    charges = jnp.clip(jax.random.uniform(own_keys[4], (N_GX, N_GY, ATOM_DEV), jnp.float32, -1.0, 1.0) * levels(own_keys[4], (N_GX, N_GY, ATOM_DEV), ((0, 4), (1, 4)), -0.4, 0.0), -1.0, 1.0)
    owners_keys = jax.random.split(jax.random.fold_in(own_keys[5], 1), N_GX * N_GY * ATOM_DEV // ATOM_DEV)
    owners_turns = jax.random.permutation(jax.random.fold_in(own_keys[5], 3), N_GX * N_GY * ATOM_DEV // ATOM_DEV)
    owners = jax.vmap(lambda own, number: routed_block(jax.random.fold_in(own_keys[5], 2), own, number, ATOM_DEV, N_GX, 1, CAP, 1))(owners_keys, owners_turns).reshape((N_GX, N_GY, ATOM_DEV, 1))
    return {"right_side": right_side, "dielectric": dielectric, "screening": screening, "weights": weights, "charges": charges, "owners": owners}


OMEGA = 0.8


def neighbour_cells(padded):
    return (padded[:-2, 1:-1, 1:-1], padded[2:, 1:-1, 1:-1],
            padded[1:-1, :-2, 1:-1], padded[1:-1, 2:, 1:-1],
            padded[1:-1, 1:-1, :-2], padded[1:-1, 1:-1, 2:])


def coefficients(dielectric_level, screen_level, factor):
    padded = jnp.pad(dielectric_level, 1)
    centre = padded[1:-1, 1:-1, 1:-1]
    face_terms = tuple(0.5 * (centre + beside) * factor for beside in neighbour_cells(padded))
    diagonal = face_terms[0] + face_terms[1] + face_terms[2] + face_terms[3] + face_terms[4] + face_terms[5] + screen_level
    return face_terms, diagonal


def apply_operator(field, coeffs):
    face_terms, diagonal = coeffs
    padded = jnp.pad(field, 1)
    cells_near = neighbour_cells(padded)
    summed = face_terms[0] * cells_near[0]
    for weight_term, cell_term in zip(face_terms[1:], cells_near[1:]):
        summed = summed + weight_term * cell_term
    return diagonal * field - summed


def sweep(field, source, coeffs):
    return field + OMEGA * (source - apply_operator(field, coeffs)) / coeffs[1]


def first_sweep(source, coeffs):
    return OMEGA * source / coeffs[1]


def restrict(field):
    shaped = field.reshape(field.shape[0] // 2, 2, field.shape[1] // 2, 2, field.shape[2] // 2, 2)
    return shaped.mean(axis=(1, 3, 5))


def prolong(field):
    return jnp.repeat(jnp.repeat(jnp.repeat(field, 2, axis=0), 2, axis=1), 2, axis=2)


def level_down(source, coeffs):
    field = first_sweep(source, coeffs)
    for repeat in range(PRE_SWEEPS - 1):
        field = sweep(field, source, coeffs)
    residual = source - apply_operator(field, coeffs)
    return field, restrict(residual)


def level_up(field, source, coeffs):
    for repeat in range(POST_SWEEPS):
        field = sweep(field, source, coeffs)
    return field


def pack_slots(force_block, owner_row):
    owner_hot = (owner_row[:, None] == jnp.arange(N_GX, dtype=jnp.int32)[None, :]).astype(jnp.int32)
    prior_count = jnp.sum((jnp.cumsum(owner_hot, axis=0, dtype=jnp.int32) - owner_hot) * owner_hot, axis=1, dtype=jnp.int32)
    target = owner_row * CAP + prior_count
    placing = (target[:, None] == jnp.arange(N_GX * CAP, dtype=jnp.int32)[None, :]).astype(jnp.float32)
    packed = jnp.dot(force_block, placing, precision=lax.Precision.HIGHEST)
    return packed.reshape(3, N_GX, CAP).transpose(1, 0, 2)


def reference(right_side, dielectric, screening, weights, charges, owners):
    dielectric_fine = dielectric.astype(jnp.float32)
    screen_fine = screening.astype(jnp.float32)
    coeffs_fine = coefficients(dielectric_fine, screen_fine, 1.0)
    dielectric_mid = restrict(dielectric_fine)
    screen_mid = restrict(screen_fine)
    coeffs_mid = coefficients(dielectric_mid, screen_mid, 0.25)
    dielectric_low = restrict(dielectric_mid)
    screen_low = restrict(screen_mid)
    coeffs_low = coefficients(dielectric_low, screen_low, 0.0625)
    fine_field, source_mid = level_down(right_side, coeffs_fine)
    mid_field, source_low = level_down(source_mid, coeffs_mid)
    low_field = first_sweep(source_low, coeffs_low)
    for repeat in range(COARSE_SWEEPS - 1):
        low_field = sweep(low_field, source_low, coeffs_low)
    mid_field = level_up(mid_field + prolong(low_field), source_mid, coeffs_mid)
    potential = level_up(fine_field + prolong(mid_field), right_side, coeffs_fine)
    padded = jnp.pad(potential, 1)
    gradient = jnp.stack([
        (padded[2:, 1:-1, 1:-1] - padded[:-2, 1:-1, 1:-1]) * 0.5,
        (padded[1:-1, 2:, 1:-1] - padded[1:-1, :-2, 1:-1]) * 0.5,
        (padded[1:-1, 1:-1, 2:] - padded[1:-1, 1:-1, :-2]) * 0.5]).astype(jnp.bfloat16)
    cell_blocks = gradient.reshape(3, N_GX, CX, N_GY, CY, NB, BZ).transpose(1, 3, 5, 0, 2, 4, 6)
    cell_blocks = cell_blocks.reshape(N_GX, N_GY, NB, 3, BLOCK_CELLS)

    def per_row(pair):
        cell_rows, weight_rows = pair
        return jnp.einsum("jbkc,jbsc->jbks", cell_rows.astype(jnp.float32), weight_rows.astype(jnp.float32))

    interpolated = lax.map(per_row, (cell_blocks, weights))
    interpolated = interpolated.transpose(0, 1, 3, 2, 4).reshape(N_GX, N_GY, 3, ATOM_DEV)
    forces = -charges[:, :, None, :] * interpolated
    packed = jax.vmap(jax.vmap(pack_slots))(forces, owners[..., 0])
    atom_forces = packed.transpose(2, 1, 0, 3, 4)
    return potential, atom_forces
```

```python
import jax
import jax.numpy as jnp
from jax import lax
from jax.experimental import pallas as pl
from jax.experimental.pallas import tpu as pltpu
from jax.sharding import PartitionSpec as P

POST_SWEEPS = 2
COARSE_SWEEPS = 6
OMEGA = 0.8
MESH = pl.DeviceIdType.MESH
F32 = jnp.float32
HX = 5
HY = 8
DIRS = tuple((dx, dy) for dx in (-1, 0, 1) for dy in (-1, 0, 1) if (dx, dy) != (0, 0))


def turn(a, shift, axis):
    return pltpu.roll(a, shift % a.shape[axis], axis)


def each(lo, hi, body, step=1):
    count = hi - lo
    step = step if count % step == 0 else 1

    def group(i, carry):
        for j in range(step):
            body(lo + i * step + j)
        return carry

    lax.fori_loop(0, count // step, group, 0)


def lanes_of(shape):
    return lax.broadcasted_iota(jnp.int32, shape, len(shape) - 1)


def rows_of(shape):
    return lax.broadcasted_iota(jnp.int32, shape, len(shape) - 2)


def coefficients(e_ref, screen, c_ref, lo, hi, factor, dup, inside, closed, step=1):
    def plane(p):
        e = e_ref[p]
        lane = lanes_of(e.shape)
        row = rows_of(e.shape)
        low_z, high_z = lane < dup, lane >= e.shape[1] - dup
        near = [e_ref[p - 1], e_ref[p + 1], turn(e, 1, 0), turn(e, -1, 0)]
        if closed:
            low_y, high_y = row < 1, row >= e.shape[0] - 1
            near[2] = jnp.where(low_y, 0.0, near[2])
            near[3] = jnp.where(high_y, 0.0, near[3])
        near.append(jnp.where(low_z, 0.0, turn(e, dup, 1)))
        near.append(jnp.where(high_z, 0.0, turn(e, -dup, 1)))
        faces = [(0.5 * factor) * (e + other) for other in near]
        diagonal = faces[0] + faces[1] + faces[2] + faces[3] + faces[4] + faces[5] + screen(p)
        if closed:
            faces[2] = jnp.where(low_y, 0.0, faces[2])
            faces[3] = jnp.where(high_y, 0.0, faces[3])
        faces[4] = jnp.where(low_z, 0.0, faces[4])
        faces[5] = jnp.where(high_z, 0.0, faces[5])
        for k in range(6):
            c_ref[k, p] = faces[k]
        c_ref[6, p] = diagonal
        ratio = OMEGA / diagonal
        c_ref[7, p] = ratio if inside is None else jnp.where(inside(p, row), ratio, 0.0)

    each(lo, hi, plane, step)


def residual(v_ref, source, c_ref, p, dup):
    v = v_ref[p]
    summed = (
        c_ref[0, p] * v_ref[p - 1]
        + c_ref[1, p] * v_ref[p + 1]
        + c_ref[2, p] * turn(v, 1, 0)
        + c_ref[3, p] * turn(v, -1, 0)
        + c_ref[4, p] * turn(v, dup, 1)
        + c_ref[5, p] * turn(v, -dup, 1)
    )
    return v, source(p) - (c_ref[6, p] * v - summed)


def first_sweep(v_ref, source, c_ref, lo, hi, step=1):
    def plane(p):
        v_ref[p] = source(p) * c_ref[7, p]

    each(lo, hi, plane, step)


def sweep(v_ref, out_ref, source, c_ref, lo, hi, dup, step=1):
    def plane(p):
        v, rest = residual(v_ref, source, c_ref, p, dup)
        out_ref[p] = v + c_ref[7, p] * rest

    each(lo, hi, plane, step)


def restrict(pair, t_ref, slot, dup):
    lane = lanes_of(pair.shape)
    pair = pair + jnp.where(lane % (2 * dup) < dup, turn(pair, -dup, 1), turn(pair, dup, 1))
    count = pair.shape[0] // 2
    t_ref[slot, pl.ds(0, 2 * count), :] = pair
    even = t_ref[slot, pl.ds(0, count, stride=2), :]
    odd = t_ref[slot, pl.ds(1, count, stride=2), :]
    return (even + odd) * 0.125


def kernel(ngx, ngy, rhs, eps, scr, wts, chg, own, pot, atoms,
           e0, f0, s0, c0, va, vb, vc, t0,
           es1, e1, s1, f1, c1, ua, ub, uw, t1,
           g2es, g2f, e2, s2, f2, c2, xa, xb, u2, t2,
           grad, sb, rb,
           sem_s0, sem_r0, sem_s1, sem_r1, sem_s2, sem_r2, sem_s3, sem_r3):
    cx, cy, nz = rhs.shape
    mx, my = cx // 2, cy // 2
    lx, ly = mx // 2, my // 2
    gx, gy = lax.axis_index("gx"), lax.axis_index("gy")
    total = ngx * ngy

    def peer(k):
        return lax.rem(gx + k // ngy, ngx), lax.rem(gy + lax.rem(k, ngy), ngy)

    def fill(ref, value):
        def plane(p):
            ref[p] = jnp.full(ref.shape[1:], value, F32)
        each(0, ref.shape[0], plane)

    fill(e0, 0.0)
    fill(f0, 0.0)
    fill(s0, 1.0)
    fill(es1, 0.0)
    fill(f1, 0.0)
    fill(uw, 0.0)

    def stage(p):
        e0[HX + p, pl.ds(HY, cy), :] = eps[p].astype(F32)
        s0[HX + p, pl.ds(HY, cy), :] = scr[p].astype(F32)
        f0[HX + p, pl.ds(HY, cy), :] = rhs[p]
    each(0, cx, stage)

    barrier = pltpu.get_barrier_semaphore()

    def greet(k, carry):
        px, py = peer(k)
        pl.semaphore_signal(barrier, inc=1, device_id={"gx": px, "gy": py}, device_id_type=MESH)
        return carry
    lax.fori_loop(1, total, greet, 0)
    pl.semaphore_wait(barrier, total - 1)

    sent = []

    def exchange(ref, base, own_x, halo_x, rows, sems, at, span):
        pending = []
        for number, (dx, dy) in enumerate(DIRS):
            limits = span(dx, dy)
            if limits is None:
                continue
            first, last = limits
            if dx == 0:
                src_x, dst_x, planes = halo_x, halo_x, own_x
            elif dx > 0:
                planes = last - first
                src_x, dst_x = halo_x + own_x - last, halo_x - last
            else:
                planes = last - first
                src_x, dst_x = halo_x + first, halo_x + own_x + first
            if dy == 0:
                src_y, dst_y, height = HY, HY, rows
            elif dy > 0:
                src_y, dst_y, height = rows, 0, HY
            else:
                src_y, dst_y, height = HY, HY + rows, HY
            target_ok = (gx + dx >= 0) & (gx + dx < ngx) & (gy + dy >= 0) & (gy + dy < ngy)
            source_ok = (gx - dx >= 0) & (gx - dx < ngx) & (gy - dy >= 0) & (gy - dy < ngy)

            def make(dx=dx, dy=dy, src_x=src_x, dst_x=dst_x, planes=planes,
                     src_y=src_y, dst_y=dst_y, height=height, number=number):
                return pltpu.make_async_remote_copy(
                    src_ref=ref.at[pl.ds(src_x, planes), pl.ds(src_y, height), :],
                    dst_ref=ref.at[pl.ds(dst_x, planes), pl.ds(dst_y, height), :],
                    send_sem=sems[0].at[at, number],
                    recv_sem=sems[1].at[at, number],
                    device_id={"gx": gx + dx, "gy": gy + dy},
                    device_id_type=MESH,
                )

            @pl.when(target_ok)
            def _(make=make):
                make().start()

            sent.append((target_ok, make))
            pending.append((source_ok, make))

        def wait():
            for ok, make in pending:
                @pl.when(ok)
                def _(make=make):
                    make().wait_recv()
        return wait

    def gather(ref, sems, at):
        def make(k):
            px, py = peer(k)
            spot = ref.at[gx, pl.ds(pl.multiple_of(gy * ly, ly), ly), :]
            return pltpu.make_async_remote_copy(
                src_ref=spot, dst_ref=spot,
                send_sem=sems[0].at[at, k], recv_sem=sems[1].at[at, k],
                device_id={"gx": px, "gy": py}, device_id_type=MESH,
            )

        def start(k, carry):
            make(k).start()
            return carry

        def finish(k, carry):
            make(k).wait_recv()
            return carry

        def release(k, carry):
            make(k).wait_send()
            return carry
        lax.fori_loop(1, total, start, 0)
        return (lambda: lax.fori_loop(1, total, finish, 0)), (
            lambda: lax.fori_loop(1, total, release, 0))

    fine = (sem_s0, sem_r0)
    early_e = exchange(e0, 0, cx, HX, cy, fine, 0, lambda dx, dy: (0, 3))
    early_f = exchange(f0, 0, cx, HX, cy, fine, 1, lambda dx, dy: (0, 2))
    early_s = exchange(s0, 0, cx, HX, cy, fine, 2, lambda dx, dy: (0, 2))

    def coarsen(i):
        pe = e0[HX + 2 * i, pl.ds(HY, cy), :] + e0[HX + 2 * i + 1, pl.ds(HY, cy), :]
        ps = s0[HX + 2 * i, pl.ds(HY, cy), :] + s0[HX + 2 * i + 1, pl.ds(HY, cy), :]
        me, ms = restrict(pe, t0, 0, 1), restrict(ps, t0, 1, 1)
        e1[mx + i, pl.ds(HY, my), :] = me
        s1[mx + i, pl.ds(HY, my), :] = ms
        es1[mx + i, pl.ds(HY, my), :] = jnp.where(lanes_of(me.shape) % 2 == 0, me, ms)
    for i in range(mx):
        coarsen(i)
    packed = []
    for ref in (e1, s1):
        for i in range(lx):
            pair = (ref[mx + 2 * i, pl.ds(HY, my), :] + ref[mx + 2 * i + 1, pl.ds(HY, my), :])
            packed.append(restrict(pair, t1, len(packed), 2))
    lane4 = lanes_of((ly, nz)) % 4
    g2es[gx, pl.ds(pl.multiple_of(gy * ly, ly), ly), :] = jnp.where(
        lane4 == 0, packed[0],
        jnp.where(lane4 == 1, packed[1], jnp.where(lane4 == 2, packed[2], packed[3])))

    mid = (sem_s1, sem_r1)
    wait_es1 = exchange(es1, 0, mx, mx, my, mid, 0, lambda dx, dy: (0, mx))
    low = (sem_s2, sem_r2)
    wait_g2es, free_g2es = gather(g2es, low, 0)
    late_e = exchange(e0, 0, cx, HX, cy, fine, 3,
                      lambda dx, dy: None if dx == 0 else ((3, 4) if dy else (3, 5)))
    late_f = exchange(f0, 0, cx, HX, cy, fine, 4,
                      lambda dx, dy: None if dx == 0 else ((2, 3) if dy else (2, 4)))
    late_s = exchange(s0, 0, cx, HX, cy, fine, 5,
                      lambda dx, dy: None if dx == 0 else ((2, 3) if dy else (2, 4)))

    peers, atom_count = ngx, own.shape[2]
    capacity = 2 * atom_count // peers
    owner = own[0, 0]
    lane = lanes_of((atom_count, nz))
    hot = (owner == lane).astype(F32)
    before = (lanes_of((atom_count, atom_count)) < rows_of((atom_count, atom_count))).astype(F32)
    prior = jnp.dot(before, hot, preferred_element_type=F32)
    place = jnp.sum(prior * hot, axis=1, keepdims=True).astype(jnp.int32) + owner * capacity
    placing = (place == lane).astype(F32)
    diag_mask = lanes_of((atom_count, atom_count)) == rows_of((atom_count, atom_count))
    charge = jnp.sum(jnp.where(diag_mask, chg[0], 0.0), axis=1, keepdims=True)

    def inside0(p, row):
        x = gx * cx + p - HX
        y = gy * cy + row - HY
        x_ok = jnp.where((x >= 0) & (x < ngx * cx), 1, 0)
        return (y >= 0) & (y < ngy * cy) & (row * 0 + x_ok > 0)

    def inside1(p, row):
        x = gx * mx + p - mx
        y = gy * my + row - HY
        x_ok = jnp.where((x >= 0) & (x < ngx * mx), 1, 0)
        return (y >= 0) & (y < ngy * my) & (row * 0 + x_ok > 0)

    rhs0 = lambda p: f0[p]
    top = HX + cx
    early_e()
    early_s()
    early_f()
    coefficients(e0, lambda p: s0[p], c0, HX - 2, top + 2, 1.0, 1, inside0, False)
    first_sweep(va, rhs0, c0, HX - 2, top + 2)
    sweep(va, vb, rhs0, c0, HX - 1, top + 1, 1)

    def down(i):
        _, r0 = residual(vb, rhs0, c0, HX + 2 * i, 1)
        _, r1 = residual(vb, rhs0, c0, HX + 2 * i + 1, 1)
        f1[mx + i, pl.ds(HY, my), :] = restrict((r0 + r1)[HY:HY + cy], t0, i, 1)
    each(0, mx, down, mx)

    wait_f1 = exchange(f1, 0, mx, mx, my, mid, 1, lambda dx, dy: (0, 2 if dx and dy else 3))

    wait_es1()

    def split(p):
        both = es1[p]
        even = lanes_of(both.shape) % 2 == 0
        e1[p] = jnp.where(even, both, turn(both, 1, 1))
        s1[p] = jnp.where(even, turn(both, -1, 1), both)
    each(0, 3 * mx, split)
    src1 = lambda p: f1[p]
    coefficients(e1, lambda p: jnp.where(s1[p] > 0.0, s1[p], 1.0), c1, 1, 3 * mx - 1, 0.25, 2,
                 inside1, False)
    wait_f1()
    first_sweep(ua, src1, c1, mx - 2, 2 * mx + 2)
    sweep(ua, ub, src1, c1, mx - 1, 2 * mx + 1, 2)
    parts = []
    for i in range(lx):
        _, r0 = residual(ub, src1, c1, mx + 2 * i, 2)
        _, r1 = residual(ub, src1, c1, mx + 2 * i + 1, 2)
        parts.append(restrict((r0 + r1)[HY:HY + my], t1, i, 2))
    g2f[gx, pl.ds(pl.multiple_of(gy * ly, ly), ly), :] = jnp.where(lane4 < 2, parts[0], parts[1])
    wait_g2f, free_g2f = gather(g2f, low, 1)
    for i in range(mx):
        uw[mx + i, pl.ds(HY, my), :] = ub[mx + i, pl.ds(HY, my), :]
    wait_uw = exchange(uw, 0, mx, mx, my, mid, 2, lambda dx, dy: (0, mx))

    wait_g2es()
    rows_low = ngy * ly
    planes_low = ngx * lx
    for ref in (e2, xa, xb):
        ref[0] = jnp.zeros((rows_low, nz), F32)
        ref[planes_low + 1] = jnp.zeros((rows_low, nz), F32)
    quad = lanes_of((rows_low, nz)) % 4

    def spread(both, which):
        alone = jnp.where(quad == which, both, 0.0)
        twice = alone + turn(alone, 1 if which % 2 == 0 else -1, 1)
        return twice + turn(twice, 2 if which < 2 else -2, 1)

    def unpack(g):
        both = g2es[g]
        for i in range(lx):
            e2[1 + lx * g + i] = spread(both, i)
            s2[1 + lx * g + i] = spread(both, lx + i)
    each(0, ngx, unpack)
    coefficients(e2, lambda p: s2[p], c2, 1, planes_low + 1, 0.0625, 4, None, True)

    late_e()
    late_f()
    late_s()
    for lo, hi in ((HX - 4, HX - 2), (top + 2, top + 4)):
        coefficients(e0, lambda p: s0[p], c0, lo, hi, 1.0, 1, inside0, False)
        first_sweep(va, rhs0, c0, lo, hi)
    sweep(va, vb, rhs0, c0, HX - 3, HX - 1, 1)
    sweep(va, vb, rhs0, c0, top + 1, top + 3, 1)
    fill(u2, 0.0)

    wait_g2f()

    def source2(g):
        both = g2f[g]
        f2[1 + lx * g] = jnp.where(quad < 2, both, turn(both, 2, 1))
        f2[2 + lx * g] = jnp.where(quad < 2, turn(both, -2, 1), both)
    each(0, ngx, source2, 2)
    src2 = lambda p: f2[p]
    first_sweep(xa, src2, c2, 1, planes_low + 1, 4)
    here, there = xa, xb
    for _ in range(COARSE_SWEEPS - 1):
        sweep(here, there, src2, c2, 1, planes_low + 1, 4, 4)
        here, there = there, here
    for_u2 = here

    def keep(p):
        u2[2 + p, pl.ds(HY, rows_low), :] = for_u2[1 + p]
    each(0, planes_low, keep, 4)

    wait_uw()
    for i in range(3 * lx):
        near = u2[lx * gx + i, pl.ds(pl.multiple_of(gy * ly, ly), 3 * ly), :]
        near = near[ly // 2:ly // 2 + 2 * ly]
        t2[pl.ds(0, 2 * ly, stride=2), :] = near
        t2[pl.ds(1, 2 * ly, stride=2), :] = near
        child = t2[...]
        ua[2 * i] = uw[2 * i] + child
        ua[2 * i + 1] = uw[2 * i + 1] + child
    sweep(ua, ub, src1, c1, 1, 3 * mx - 1, 2, 2)
    sweep(ub, ua, src1, c1, 2, 3 * mx - 2, 2, 2)

    for c in range(mx - 2, 2 * mx + 2):
        near = ua[c][HY // 2:HY // 2 + (cy + 2 * HY) // 2]
        count = near.shape[0]
        t0[c - mx + 2, pl.ds(0, count, stride=2), :] = near
        t0[c - mx + 2, pl.ds(1, count, stride=2), :] = near
        child = t0[c - mx + 2]
        for p in (HX + 2 * (c - mx), HX + 2 * (c - mx) + 1):
            if HX - 3 <= p < top + 3:
                va[p] = vb[p] + child
    sweep(va, vc, rhs0, c0, HX - 2, top + 2, 1)
    sweep(vc, va, rhs0, c0, HX - 1, top + 1, 1)

    lane = lanes_of((cy // 8, 8, nz))
    row = rows_of((cy // 8, 8, nz))

    def swap(a):
        for bit in (1, 2, 4):
            r, g = (row // bit) % 2, (lane // (16 * bit)) % 2
            one = turn(turn(a, -bit, 1), 16 * bit, 2)
            other = one if bit == 4 else turn(turn(a, bit, 1), -16 * bit, 2)
            a = jnp.where(r == g, a, jnp.where(r == 0, one, other))
        return a

    def atoms_of(x, sums):
        p = HX + x
        v = va[p]
        pot[x] = v[HY:HY + cy]
        lane_v = lanes_of(v.shape)
        up = jnp.where(lane_v == nz - 1, 0.0, turn(v, -1, 1))
        down_z = jnp.where(lane_v == 0, 0.0, turn(v, 1, 1))
        steps = ((va[p + 1] - va[p - 1]) * 0.5,
                 (turn(v, -1, 0) - turn(v, 1, 0)) * 0.5,
                 (up - down_z) * 0.5)
        tiles = [swap(g[HY:HY + cy].astype(jnp.bfloat16).astype(F32).reshape(cy // 8, 8, nz))
                 for g in steps]
        sums = list(sums)
        for q in range(cy // 8):
            at = pl.multiple_of(x * (cy * 16) + q * nz, nz)
            w = wts[0, 0, :, :, pl.ds(at, nz)].astype(F32)
            for k in range(3):
                sums[k] = sums[k] + w * tiles[k][q][:, None, :]
        return tuple(sums)

    blocks, slots = wts.shape[2], wts.shape[3]
    zero = jnp.zeros((blocks, slots, nz), F32)
    sums = lax.fori_loop(0, cx, atoms_of, (zero, zero, zero))
    row8 = rows_of((8, nz))
    result = jnp.zeros((8, nz), F32)
    for k in range(3):
        force = -charge * jnp.sum(sums[k].reshape(blocks * slots, nz), axis=1, keepdims=True)
        line = jnp.sum(force * placing, axis=0, keepdims=True)
        result = jnp.where(row8 == k, line, result)
    for t in range(peers):
        sb[t] = turn(result, -t * capacity, 1)

    def to_owner(o):
        target = lax.rem(gx + o, peers)
        return pltpu.make_async_remote_copy(
            src_ref=sb.at[target], dst_ref=rb.at[gx],
            send_sem=sem_s3.at[o], recv_sem=sem_r3.at[o],
            device_id={"gx": target, "gy": gy}, device_id_type=MESH)
    for o in range(1, peers):
        to_owner(o).start()
    rb[gx] = sb[gx]
    for ok, make in sent:
        @pl.when(ok)
        def _(make=make):
            make().wait_send()
    free_g2es()
    free_g2f()
    for o in range(1, peers):
        to_owner(o).wait_recv()
    for t in range(peers):
        atoms[0, 0, t] = rb[t][:3, :capacity]
    for o in range(1, peers):
        to_owner(o).wait_send()


def solution(mesh):
    ngx, ngy = mesh.shape["gx"], mesh.shape["gy"]

    def shards(right_side, dielectric, screening, weights, charges, owners):
        cx, cy, nz = right_side.shape
        capacity = 2 * owners.shape[2] // ngx
        vmem = lambda *shape: pltpu.VMEM(shape, F32)
        x0, y0 = cx + 2 * HX, cy + 2 * HY
        mx, my = cx // 2, cy // 2
        x1, y1 = 3 * mx, my + 2 * HY
        lx, ly = mx // 2, my // 2
        x2, y2 = ngx * lx, ngy * ly
        w0, w1, w2 = (x0, y0, nz), (x1, y1, nz), (x2 + 2, y2, nz)
        scratch = [
            vmem(*w0), vmem(*w0), vmem(*w0), vmem(8, *w0), vmem(*w0), vmem(*w0), vmem(*w0),
            vmem(mx + 4, y0, nz),
            vmem(*w1), vmem(*w1), vmem(*w1), vmem(*w1), vmem(8, *w1), vmem(*w1), vmem(*w1),
            vmem(*w1), vmem(4, my, nz),
            vmem(ngx, y2, nz), vmem(ngx, y2, nz), vmem(*w2), vmem(*w2), vmem(*w2),
            vmem(8, *w2), vmem(*w2), vmem(*w2), vmem(x2 + 4, y2 + 2 * HY, nz), vmem(4 * ly, nz),
            vmem(8, nz), vmem(ngx, 8, nz), vmem(ngx, 8, nz),
            pltpu.SemaphoreType.DMA((6, 8)), pltpu.SemaphoreType.DMA((6, 8)),
            pltpu.SemaphoreType.DMA((3, 8)), pltpu.SemaphoreType.DMA((3, 8)),
            pltpu.SemaphoreType.DMA((2, ngx * ngy)), pltpu.SemaphoreType.DMA((2, ngx * ngy)),
            pltpu.SemaphoreType.DMA((ngx,)), pltpu.SemaphoreType.DMA((ngx,)),
        ]

        def body(*refs):
            kernel(ngx, ngy, *refs)

        return pl.pallas_call(
            body,
            out_shape=(
                jax.ShapeDtypeStruct((cx, cy, nz), F32),
                jax.ShapeDtypeStruct((1, 1, ngx, 3, capacity), F32),
            ),
            in_specs=[pl.BlockSpec(memory_space=pltpu.VMEM)] * 6,
            out_specs=(pl.BlockSpec(memory_space=pltpu.VMEM),) * 2,
            scratch_shapes=scratch,
            compiler_params=pltpu.CompilerParams(
                collective_id=0, has_side_effects=True, vmem_limit_bytes=60 * 2**20
            ),
        )(right_side, dielectric, screening, weights, charges, owners)

    in_specs = (
        P(("rep", "gx"), "gy", None),
        P(("rep", "gx"), "gy", None),
        P(("rep", "gx"), "gy", None),
        P(("rep", "gx"), "gy", None, None, None),
        P(("rep", "gx"), "gy", None),
        P(("rep", "gx"), "gy", None, None),
    )
    out_specs = (P(("rep", "gx"), "gy", None), P(("rep", "gx"), "gy", None, None, None))
    return jax.shard_map(shards, mesh=mesh, in_specs=in_specs, out_specs=out_specs, check_vma=False)
```

```python
import jax
import jax.numpy as jnp
from jax import lax
from jax.experimental import pallas as pl
from jax.experimental.pallas import tpu as pltpu
from jax.sharding import PartitionSpec as P

POST_SWEEPS = 2
COARSE_SWEEPS = 6
OMEGA = 0.8
MESH = pl.DeviceIdType.MESH
F32 = jnp.float32
HX = 5
HY = 8
DIRS = tuple((dx, dy) for dx in (-1, 0, 1) for dy in (-1, 0, 1) if (dx, dy) != (0, 0))


def turn(a, shift, axis):
    return pltpu.roll(a, shift % a.shape[axis], axis)


def each(lo, hi, body, step=1):
    count = hi - lo
    step = step if count % step == 0 else 1

    def group(i, carry):
        for j in range(step):
            body(lo + i * step + j)
        return carry

    lax.fori_loop(0, count // step, group, 0)


def lanes_of(shape):
    return lax.broadcasted_iota(jnp.int32, shape, len(shape) - 1)


def rows_of(shape):
    return lax.broadcasted_iota(jnp.int32, shape, len(shape) - 2)


def coefficients(e_ref, screen, c_ref, lo, hi, factor, dup, inside, closed, step=1):
    def plane(p):
        e = e_ref[p]
        lane = lanes_of(e.shape)
        row = rows_of(e.shape)
        low_z, high_z = lane < dup, lane >= e.shape[1] - dup
        near = [e_ref[p - 1], e_ref[p + 1], turn(e, 1, 0), turn(e, -1, 0)]
        if closed:
            low_y, high_y = row < 1, row >= e.shape[0] - 1
            near[2] = jnp.where(low_y, 0.0, near[2])
            near[3] = jnp.where(high_y, 0.0, near[3])
        near.append(jnp.where(low_z, 0.0, turn(e, dup, 1)))
        near.append(jnp.where(high_z, 0.0, turn(e, -dup, 1)))
        faces = [(0.5 * factor) * (e + other) for other in near]
        diagonal = faces[0] + faces[1] + faces[2] + faces[3] + faces[4] + faces[5] + screen(p)
        if closed:
            faces[2] = jnp.where(low_y, 0.0, faces[2])
            faces[3] = jnp.where(high_y, 0.0, faces[3])
        faces[4] = jnp.where(low_z, 0.0, faces[4])
        faces[5] = jnp.where(high_z, 0.0, faces[5])
        for k in range(6):
            c_ref[k, p] = faces[k]
        c_ref[6, p] = diagonal
        ratio = OMEGA / diagonal
        c_ref[7, p] = ratio if inside is None else jnp.where(inside(p, row), ratio, 0.0)

    each(lo, hi, plane, step)


def residual(v_ref, source, c_ref, p, dup):
    v = v_ref[p]
    summed = (
        c_ref[0, p] * v_ref[p - 1]
        + c_ref[1, p] * v_ref[p + 1]
        + c_ref[2, p] * turn(v, 1, 0)
        + c_ref[3, p] * turn(v, -1, 0)
        + c_ref[4, p] * turn(v, dup, 1)
        + c_ref[5, p] * turn(v, -dup, 1)
    )
    return v, source(p) - (c_ref[6, p] * v - summed)


def first_sweep(v_ref, source, c_ref, lo, hi, step=1):
    def plane(p):
        v_ref[p] = source(p) * c_ref[7, p]

    each(lo, hi, plane, step)


def sweep(v_ref, out_ref, source, c_ref, lo, hi, dup, step=1):
    def plane(p):
        v, rest = residual(v_ref, source, c_ref, p, dup)
        out_ref[p] = v + c_ref[7, p] * rest

    each(lo, hi, plane, step)


def restrict(pair, t_ref, slot, dup):
    lane = lanes_of(pair.shape)
    pair = pair + jnp.where(lane % (2 * dup) < dup, turn(pair, -dup, 1), turn(pair, dup, 1))
    count = pair.shape[0] // 2
    t_ref[slot, pl.ds(0, 2 * count), :] = pair
    even = t_ref[slot, pl.ds(0, count, stride=2), :]
    odd = t_ref[slot, pl.ds(1, count, stride=2), :]
    return (even + odd) * 0.125


def kernel(ngx, ngy, rhs, eps_in, scr_in, wts_in, chg_in, own_in, pot, atoms,
           eps, scr, wts, chg, own, sem_in,
           e0, f0, s0, c0, va, vb, vc, t0,
           es1, e1, s1, f1, c1, ua, ub, uw, t1,
           g2es, g2f, e2, s2, f2, c2, xa, xb, u2, t2,
           grad, sb, rb,
           hello, sem_s0, sem_r0, sem_s1, sem_r1, sem_s2, sem_r2, sem_s3, sem_r3):
    cx, cy, nz = rhs.shape
    mx, my = cx // 2, cy // 2
    lx, ly = mx // 2, my // 2
    gx, gy = lax.axis_index("gx"), lax.axis_index("gy")
    total = ngx * ngy

    def peer(k):
        return lax.rem(gx + k // ngy, ngx), lax.rem(gy + lax.rem(k, ngy), ngy)

    def fill(ref, value):
        def plane(p):
            ref[p] = jnp.full(ref.shape[1:], value, F32)
        each(0, ref.shape[0], plane)

    loads = [pltpu.make_async_copy(a, b, sem_in.at[i]) for i, (a, b) in enumerate((
        (eps_in, eps), (scr_in, scr), (wts_in, wts), (chg_in, chg), (own_in, own)))]
    for load in loads:
        load.start()

    fill(e0, 0.0)
    fill(f0, 0.0)
    fill(s0, 1.0)
    fill(es1, 0.0)
    fill(f1, 0.0)
    fill(uw, 0.0)

    load_f = pltpu.make_async_copy(
        rhs, f0.at[pl.ds(HX, cx), pl.ds(HY, cy), :], sem_in.at[5])
    load_f.start()

    def near_ok(dx, dy):
        return (gx + dx >= 0) & (gx + dx < ngx) & (gy + dy >= 0) & (gy + dy < ngy)

    def greet(sem):
        for dx, dy in DIRS:
            @pl.when(near_ok(dx, dy))
            def _(dx=dx, dy=dy):
                pl.semaphore_signal(
                    sem, inc=1, device_id={"gx": gx + dx, "gy": gy + dy}, device_id_type=MESH)

    def greeted(sem):
        wide = 3 - jnp.where(gx == 0, 1, 0) - jnp.where(gx == ngx - 1, 1, 0)
        high = 3 - jnp.where(gy == 0, 1, 0) - jnp.where(gy == ngy - 1, 1, 0)
        pl.semaphore_wait(sem, wide * high - 1)

    barrier = pltpu.get_barrier_semaphore()

    greet(barrier)
    loads[0].wait()
    loads[1].wait()

    def stage(p):
        e0[HX + p, pl.ds(HY, cy), :] = eps[p].astype(F32)
        s0[HX + p, pl.ds(HY, cy), :] = scr[p].astype(F32)
    each(0, cx, stage, 2)
    load_f.wait()
    greeted(barrier)

    sent = []

    def exchange(ref, base, own_x, halo_x, rows, sems, at, span):
        pending = []
        for number, (dx, dy) in enumerate(DIRS):
            limits = span(dx, dy)
            if limits is None:
                continue
            first, last = limits
            if dx == 0:
                src_x, dst_x, planes = halo_x, halo_x, own_x
            elif dx > 0:
                planes = last - first
                src_x, dst_x = halo_x + own_x - last, halo_x - last
            else:
                planes = last - first
                src_x, dst_x = halo_x + first, halo_x + own_x + first
            if dy == 0:
                src_y, dst_y, height = HY, HY, rows
            elif dy > 0:
                src_y, dst_y, height = rows, 0, HY
            else:
                src_y, dst_y, height = HY, HY + rows, HY
            target_ok = (gx + dx >= 0) & (gx + dx < ngx) & (gy + dy >= 0) & (gy + dy < ngy)
            source_ok = (gx - dx >= 0) & (gx - dx < ngx) & (gy - dy >= 0) & (gy - dy < ngy)

            def make(dx=dx, dy=dy, src_x=src_x, dst_x=dst_x, planes=planes,
                     src_y=src_y, dst_y=dst_y, height=height, number=number):
                return pltpu.make_async_remote_copy(
                    src_ref=ref.at[pl.ds(src_x, planes), pl.ds(src_y, height), :],
                    dst_ref=ref.at[pl.ds(dst_x, planes), pl.ds(dst_y, height), :],
                    send_sem=sems[0].at[at, number],
                    recv_sem=sems[1].at[at, number],
                    device_id={"gx": gx + dx, "gy": gy + dy},
                    device_id_type=MESH,
                )

            @pl.when(target_ok)
            def _(make=make):
                make().start()

            sent.append((target_ok, make))
            pending.append((dx, source_ok, make))

        def wait(along=None):
            for dx, ok, make in pending:
                if along is not None and (dx == 0) != (along == "y"):
                    continue

                @pl.when(ok)
                def _(make=make):
                    make().wait_recv()
        return wait

    def gather(ref, sems, at):
        def make(k):
            px, py = peer(k)
            spot = ref.at[gx, pl.ds(pl.multiple_of(gy * ly, ly), ly), :]
            return pltpu.make_async_remote_copy(
                src_ref=spot, dst_ref=spot,
                send_sem=sems[0].at[at, k], recv_sem=sems[1].at[at, k],
                device_id={"gx": px, "gy": py}, device_id_type=MESH,
            )

        def start(k, carry):
            make(k).start()
            return carry

        def finish(k, carry):
            make(k).wait_recv()
            return carry

        def release(k, carry):
            make(k).wait_send()
            return carry
        lax.fori_loop(1, total, start, 0)
        return (lambda: lax.fori_loop(1, total, finish, 0)), (
            lambda: lax.fori_loop(1, total, release, 0))

    rounds = max(ngx, ngy) - 2

    fine = (sem_s0, sem_r0)
    if rounds > 0:
        greet(hello.at[0])
    early_e = exchange(e0, 0, cx, HX, cy, fine, 0, lambda dx, dy: (0, 3))
    early_f = exchange(f0, 0, cx, HX, cy, fine, 1, lambda dx, dy: (0, 2))
    early_s = exchange(s0, 0, cx, HX, cy, fine, 2, lambda dx, dy: (0, 2))

    def coarsen(i):
        pe = e0[HX + 2 * i, pl.ds(HY, cy), :] + e0[HX + 2 * i + 1, pl.ds(HY, cy), :]
        ps = s0[HX + 2 * i, pl.ds(HY, cy), :] + s0[HX + 2 * i + 1, pl.ds(HY, cy), :]
        me, ms = restrict(pe, t0, 0, 1), restrict(ps, t0, 1, 1)
        e1[mx + i, pl.ds(HY, my), :] = me
        s1[mx + i, pl.ds(HY, my), :] = ms
        es1[mx + i, pl.ds(HY, my), :] = jnp.where(lanes_of(me.shape) % 2 == 0, me, ms)
    for i in range(mx):
        coarsen(i)
    if rounds > 0:
        def spread_word(r, carry):
            greeted(hello.at[r])
            greet(hello.at[r + 1])
            return carry
        lax.fori_loop(0, rounds - 1, spread_word, 0)
    packed = []
    for ref in (e1, s1):
        for i in range(lx):
            pair = (ref[mx + 2 * i, pl.ds(HY, my), :] + ref[mx + 2 * i + 1, pl.ds(HY, my), :])
            packed.append(restrict(pair, t1, len(packed), 2))
    lane4 = lanes_of((ly, nz)) % 4
    g2es[gx, pl.ds(pl.multiple_of(gy * ly, ly), ly), :] = jnp.where(
        lane4 == 0, packed[0],
        jnp.where(lane4 == 1, packed[1], jnp.where(lane4 == 2, packed[2], packed[3])))

    mid = (sem_s1, sem_r1)
    wait_es1 = exchange(es1, 0, mx, mx, my, mid, 0, lambda dx, dy: (0, mx))
    low = (sem_s2, sem_r2)
    if rounds > 0:
        greeted(hello.at[rounds - 1])
    wait_g2es, free_g2es = gather(g2es, low, 0)
    late_e = exchange(e0, 0, cx, HX, cy, fine, 3,
                      lambda dx, dy: None if dx == 0 else ((3, 4) if dy else (3, 5)))
    late_f = exchange(f0, 0, cx, HX, cy, fine, 4,
                      lambda dx, dy: None if dx == 0 else ((2, 3) if dy else (2, 4)))
    late_s = exchange(s0, 0, cx, HX, cy, fine, 5,
                      lambda dx, dy: None if dx == 0 else ((2, 3) if dy else (2, 4)))

    loads[3].wait()
    loads[4].wait()
    peers, atom_count = ngx, own.shape[2]
    capacity = 2 * atom_count // peers
    lane = lanes_of((atom_count, nz))
    square = lanes_of((atom_count, atom_count)) == rows_of((atom_count, atom_count))
    owner = jnp.sum(jnp.where(square, own[0], 0), axis=1, keepdims=True)
    hot = (owner == lane).astype(F32)
    before = (lanes_of((atom_count, atom_count)) < rows_of((atom_count, atom_count))).astype(F32)
    prior = jnp.dot(before, hot, preferred_element_type=F32)
    place = jnp.sum(prior * hot, axis=1, keepdims=True).astype(jnp.int32) + owner * capacity
    placing = (place == lane).astype(F32)
    charge = jnp.sum(jnp.where(square, chg[0], 0.0), axis=1, keepdims=True)

    def inside0(p, row):
        x = gx * cx + p - HX
        y = gy * cy + row - HY
        x_ok = jnp.where((x >= 0) & (x < ngx * cx), 1, 0)
        return (y >= 0) & (y < ngy * cy) & (row * 0 + x_ok > 0)

    def inside1(p, row):
        x = gx * mx + p - mx
        y = gy * my + row - HY
        x_ok = jnp.where((x >= 0) & (x < ngx * mx), 1, 0)
        return (y >= 0) & (y < ngy * my) & (row * 0 + x_ok > 0)

    rhs0 = lambda p: f0[p]
    top = HX + cx
    for early in (early_e, early_s, early_f):
        early("y")

    def begin(lo, hi, step):
        coefficients(e0, lambda p: s0[p], c0, lo, hi, 1.0, 1, inside0, False, step)
        first_sweep(va, rhs0, c0, lo, hi, step)

    begin(HX + 1, top - 1, 2)
    sweep(va, vb, rhs0, c0, HX + 2, top - 2, 1, 2)
    for early in (early_e, early_s, early_f):
        early("x")
    begin(HX - 2, HX + 1, 3)
    begin(top - 1, top + 2, 3)
    sweep(va, vb, rhs0, c0, HX - 1, HX + 2, 1, 3)
    sweep(va, vb, rhs0, c0, top - 2, top + 1, 1, 3)

    def down(i):
        _, r0 = residual(vb, rhs0, c0, HX + 2 * i, 1)
        _, r1 = residual(vb, rhs0, c0, HX + 2 * i + 1, 1)
        f1[mx + i, pl.ds(HY, my), :] = restrict((r0 + r1)[HY:HY + cy], t0, i, 1)
    each(0, mx, down, mx)

    wait_f1 = exchange(f1, 0, mx, mx, my, mid, 1, lambda dx, dy: (0, 2 if dx and dy else 3))

    wait_es1()

    def split(p):
        both = es1[p]
        even = lanes_of(both.shape) % 2 == 0
        e1[p] = jnp.where(even, both, turn(both, 1, 1))
        s1[p] = jnp.where(even, turn(both, -1, 1), both)
    each(0, 3 * mx, split, 4)
    src1 = lambda p: f1[p]
    coefficients(e1, lambda p: jnp.where(s1[p] > 0.0, s1[p], 1.0), c1, 1, 3 * mx - 1, 0.25, 2,
                 inside1, False, 2)
    wait_f1()
    first_sweep(ua, src1, c1, mx - 2, 2 * mx + 2, 4)
    sweep(ua, ub, src1, c1, mx - 1, 2 * mx + 1, 2, 3)
    parts = []
    for i in range(lx):
        _, r0 = residual(ub, src1, c1, mx + 2 * i, 2)
        _, r1 = residual(ub, src1, c1, mx + 2 * i + 1, 2)
        parts.append(restrict((r0 + r1)[HY:HY + my], t1, i, 2))
    g2f[gx, pl.ds(pl.multiple_of(gy * ly, ly), ly), :] = jnp.where(lane4 < 2, parts[0], parts[1])
    wait_g2f, free_g2f = gather(g2f, low, 1)
    for i in range(mx):
        uw[mx + i, pl.ds(HY, my), :] = ub[mx + i, pl.ds(HY, my), :]
    wait_uw = exchange(uw, 0, mx, mx, my, mid, 2, lambda dx, dy: (0, mx))

    wait_g2es()
    rows_low = ngy * ly
    planes_low = ngx * lx
    for ref in (e2, xa, xb):
        ref[0] = jnp.zeros((rows_low, nz), F32)
        ref[planes_low + 1] = jnp.zeros((rows_low, nz), F32)
    quad = lanes_of((rows_low, nz)) % 4

    def spread(both, which):
        alone = jnp.where(quad == which, both, 0.0)
        twice = alone + turn(alone, 1 if which % 2 == 0 else -1, 1)
        return twice + turn(twice, 2 if which < 2 else -2, 1)

    def unpack(g):
        both = g2es[g]
        for i in range(lx):
            e2[1 + lx * g + i] = spread(both, i)
            s2[1 + lx * g + i] = spread(both, lx + i)
    each(0, ngx, unpack)
    coefficients(e2, lambda p: s2[p], c2, 1, planes_low + 1, 0.0625, 4, None, True, 2)

    late_e()
    late_f()
    late_s()
    for lo, hi in ((HX - 4, HX - 2), (top + 2, top + 4)):
        begin(lo, hi, 2)
    sweep(va, vb, rhs0, c0, HX - 3, HX - 1, 1, 2)
    sweep(va, vb, rhs0, c0, top + 1, top + 3, 1, 2)
    fill(u2, 0.0)

    wait_g2f()

    def source2(g):
        both = g2f[g]
        f2[1 + lx * g] = jnp.where(quad < 2, both, turn(both, 2, 1))
        f2[2 + lx * g] = jnp.where(quad < 2, turn(both, -2, 1), both)
    each(0, ngx, source2, 2)
    src2 = lambda p: f2[p]
    first_sweep(xa, src2, c2, 1, planes_low + 1, 4)
    here, there = xa, xb
    for _ in range(COARSE_SWEEPS - 1):
        sweep(here, there, src2, c2, 1, planes_low + 1, 4, 4)
        here, there = there, here
    for_u2 = here

    def keep(p):
        u2[2 + p, pl.ds(HY, rows_low), :] = for_u2[1 + p]
    each(0, planes_low, keep, 4)

    wait_uw()
    for i in range(3 * lx):
        near = u2[lx * gx + i, pl.ds(pl.multiple_of(gy * ly, ly), 3 * ly), :]
        near = near[ly // 2:ly // 2 + 2 * ly]
        t2[pl.ds(0, 2 * ly, stride=2), :] = near
        t2[pl.ds(1, 2 * ly, stride=2), :] = near
        child = t2[...]
        ua[2 * i] = uw[2 * i] + child
        ua[2 * i + 1] = uw[2 * i + 1] + child
    sweep(ua, ub, src1, c1, 1, 3 * mx - 1, 2, 2)
    sweep(ub, ua, src1, c1, 2, 3 * mx - 2, 2, 4)

    for c in range(mx - 2, 2 * mx + 2):
        near = ua[c][HY // 2:HY // 2 + (cy + 2 * HY) // 2]
        count = near.shape[0]
        t0[c - mx + 2, pl.ds(0, count, stride=2), :] = near
        t0[c - mx + 2, pl.ds(1, count, stride=2), :] = near
        child = t0[c - mx + 2]
        for p in (HX + 2 * (c - mx), HX + 2 * (c - mx) + 1):
            if HX - 3 <= p < top + 3:
                va[p] = vb[p] + child
    sweep(va, vc, rhs0, c0, HX - 2, top + 2, 1, 3)
    sweep(vc, va, rhs0, c0, HX - 1, top + 1, 1, 2)
    store = pltpu.make_async_copy(
        va.at[pl.ds(HX, cx), pl.ds(HY, cy), :], pot, sem_in.at[5])
    store.start()

    lane = lanes_of((cy // 8, 8, nz))
    row = rows_of((cy // 8, 8, nz))

    def swap(a):
        for bit in (1, 2, 4):
            r, g = (row // bit) % 2, (lane // (16 * bit)) % 2
            one = turn(turn(a, -bit, 1), 16 * bit, 2)
            other = one if bit == 4 else turn(turn(a, bit, 1), -16 * bit, 2)
            a = jnp.where(r == g, a, jnp.where(r == 0, one, other))
        return a

    def atoms_of(x, sums):
        p = HX + x
        v = va[p]
        lane_v = lanes_of(v.shape)
        up = jnp.where(lane_v == nz - 1, 0.0, turn(v, -1, 1))
        down_z = jnp.where(lane_v == 0, 0.0, turn(v, 1, 1))
        steps = ((va[p + 1] - va[p - 1]) * 0.5,
                 (turn(v, -1, 0) - turn(v, 1, 0)) * 0.5,
                 (up - down_z) * 0.5)
        tiles = [swap(g[HY:HY + cy].astype(jnp.bfloat16).astype(F32).reshape(cy // 8, 8, nz))
                 for g in steps]
        sums = list(sums)
        for q in range(cy // 8):
            at = pl.multiple_of(x * (cy * 16) + q * nz, nz)
            w = wts[0, 0, :, :, pl.ds(at, nz)].astype(F32)
            for k in range(3):
                sums[k] = sums[k] + w * tiles[k][q][:, None, :]
        return tuple(sums)

    blocks, slots = wts.shape[2], wts.shape[3]
    zero = jnp.zeros((blocks, slots, nz), F32)
    loads[2].wait()
    sums = lax.fori_loop(0, cx // 2, lambda i, carry: atoms_of(2 * i + 1, atoms_of(2 * i, carry)),
                         (zero, zero, zero))
    row8 = rows_of((8, nz))
    result = jnp.zeros((8, nz), F32)
    for k in range(3):
        force = -charge * jnp.sum(sums[k].reshape(blocks * slots, nz), axis=1, keepdims=True)
        line = jnp.sum(force * placing, axis=0, keepdims=True)
        result = jnp.where(row8 == k, line, result)
    for t in range(peers):
        sb[t] = turn(result, -t * capacity, 1)

    def to_owner(o):
        target = lax.rem(gx + o, peers)
        return pltpu.make_async_remote_copy(
            src_ref=sb.at[target], dst_ref=rb.at[gx],
            send_sem=sem_s3.at[o], recv_sem=sem_r3.at[o],
            device_id={"gx": target, "gy": gy}, device_id_type=MESH)
    for o in range(1, peers):
        to_owner(o).start()
    rb[gx] = sb[gx]
    for ok, make in sent:
        @pl.when(ok)
        def _(make=make):
            make().wait_send()
    free_g2es()
    free_g2f()
    for o in range(1, peers):
        to_owner(o).wait_recv()
    for t in range(peers):
        atoms[0, 0, t] = rb[t][:3, :capacity]
    for o in range(1, peers):
        to_owner(o).wait_send()
    store.wait()


def solution(mesh):
    ngx, ngy = mesh.shape["gx"], mesh.shape["gy"]

    def shards(right_side, dielectric, screening, weights, charges, owners):
        cx, cy, nz = right_side.shape
        capacity = 2 * owners.shape[2] // ngx
        vmem = lambda *shape: pltpu.VMEM(shape, F32)
        x0, y0 = cx + 2 * HX, cy + 2 * HY
        mx, my = cx // 2, cy // 2
        x1, y1 = 3 * mx, my + 2 * HY
        lx, ly = mx // 2, my // 2
        x2, y2 = ngx * lx, ngy * ly
        w0, w1, w2 = (x0, y0, nz), (x1, y1, nz), (x2 + 2, y2, nz)
        scratch = [
            pltpu.VMEM((cx, cy, nz), jnp.bfloat16), pltpu.VMEM((cx, cy, nz), jnp.bfloat16),
            pltpu.VMEM(weights.shape, jnp.bfloat16), vmem(*charges.shape),
            pltpu.VMEM(charges.shape, jnp.int32), pltpu.SemaphoreType.DMA((6,)),
            vmem(*w0), vmem(*w0), vmem(*w0), vmem(8, *w0), vmem(*w0), vmem(*w0), vmem(*w0),
            vmem(mx + 4, y0, nz),
            vmem(*w1), vmem(*w1), vmem(*w1), vmem(*w1), vmem(8, *w1), vmem(*w1), vmem(*w1),
            vmem(*w1), vmem(4, my, nz),
            vmem(ngx, y2, nz), vmem(ngx, y2, nz), vmem(*w2), vmem(*w2), vmem(*w2),
            vmem(8, *w2), vmem(*w2), vmem(*w2), vmem(x2 + 4, y2 + 2 * HY, nz), vmem(4 * ly, nz),
            vmem(8, nz), vmem(ngx, 8, nz), vmem(ngx, 8, nz),
            pltpu.SemaphoreType.REGULAR((max(ngx, ngy, 3) - 2,)),
            pltpu.SemaphoreType.DMA((6, 8)), pltpu.SemaphoreType.DMA((6, 8)),
            pltpu.SemaphoreType.DMA((3, 8)), pltpu.SemaphoreType.DMA((3, 8)),
            pltpu.SemaphoreType.DMA((2, ngx * ngy)), pltpu.SemaphoreType.DMA((2, ngx * ngy)),
            pltpu.SemaphoreType.DMA((ngx,)), pltpu.SemaphoreType.DMA((ngx,)),
        ]

        def body(*refs):
            kernel(ngx, ngy, *refs)

        return pl.pallas_call(
            body,
            out_shape=(
                jax.ShapeDtypeStruct((cx, cy, nz), F32),
                jax.ShapeDtypeStruct((1, 1, ngx, 3, capacity), F32),
            ),
            in_specs=[pl.BlockSpec(memory_space=pl.ANY)] * 6,
            out_specs=(pl.BlockSpec(memory_space=pl.ANY), pl.BlockSpec(memory_space=pltpu.VMEM)),
            scratch_shapes=scratch,
            compiler_params=pltpu.CompilerParams(
                collective_id=0, has_side_effects=True, vmem_limit_bytes=60 * 2**20
            ),
        )(right_side, dielectric, screening, weights, charges, owners.reshape(charges.shape))

    in_specs = (
        P(("rep", "gx"), "gy", None),
        P(("rep", "gx"), "gy", None),
        P(("rep", "gx"), "gy", None),
        P(("rep", "gx"), "gy", None, None, None),
        P(("rep", "gx"), "gy", None),
        P(("rep", "gx"), "gy", None, None),
    )
    out_specs = (P(("rep", "gx"), "gy", None), P(("rep", "gx"), "gy", None, None, None))
    return jax.shard_map(shards, mesh=mesh, in_specs=in_specs, out_specs=out_specs, check_vma=False)
```

```python
import jax
import jax.numpy as jnp
from jax import lax
from jax.experimental import pallas as pl
from jax.experimental.pallas import tpu as pltpu
from jax.sharding import PartitionSpec as P

POST_SWEEPS = 2
COARSE_SWEEPS = 6
OMEGA = 0.8
MESH = pl.DeviceIdType.MESH
F32 = jnp.float32
HX = 5
HY = 8
DIRS = tuple((dx, dy) for dx in (-1, 0, 1) for dy in (-1, 0, 1) if (dx, dy) != (0, 0))


def turn(a, shift, axis):
    return pltpu.roll(a, shift % a.shape[axis], axis)


def each(lo, hi, body, step=1):
    count = hi - lo
    step = step if count % step == 0 else 1

    def group(i, carry):
        for j in range(step):
            body(lo + i * step + j)
        return carry

    lax.fori_loop(0, count // step, group, 0)


def lanes_of(shape):
    return lax.broadcasted_iota(jnp.int32, shape, len(shape) - 1)


def rows_of(shape):
    return lax.broadcasted_iota(jnp.int32, shape, len(shape) - 2)


def coefficients(e_ref, screen, c_ref, lo, hi, factor, dup, inside, closed, step=1):
    def plane(p):
        e = e_ref[p]
        lane = lanes_of(e.shape)
        row = rows_of(e.shape)
        low_z, high_z = lane < dup, lane >= e.shape[1] - dup
        near = [e_ref[p - 1], e_ref[p + 1], turn(e, 1, 0), turn(e, -1, 0)]
        if closed:
            low_y, high_y = row < 1, row >= e.shape[0] - 1
            near[2] = jnp.where(low_y, 0.0, near[2])
            near[3] = jnp.where(high_y, 0.0, near[3])
        near.append(jnp.where(low_z, 0.0, turn(e, dup, 1)))
        near.append(jnp.where(high_z, 0.0, turn(e, -dup, 1)))
        faces = [(0.5 * factor) * (e + other) for other in near]
        diagonal = faces[0] + faces[1] + faces[2] + faces[3] + faces[4] + faces[5] + screen(p)
        if closed:
            faces[2] = jnp.where(low_y, 0.0, faces[2])
            faces[3] = jnp.where(high_y, 0.0, faces[3])
        faces[4] = jnp.where(low_z, 0.0, faces[4])
        faces[5] = jnp.where(high_z, 0.0, faces[5])
        for k in range(6):
            c_ref[k, p] = faces[k]
        c_ref[6, p] = diagonal
        ratio = OMEGA / diagonal
        c_ref[7, p] = ratio if inside is None else jnp.where(inside(p, row), ratio, 0.0)

    each(lo, hi, plane, step)


def residual(v_ref, source, c_ref, p, dup):
    v = v_ref[p]
    summed = (
        c_ref[0, p] * v_ref[p - 1]
        + c_ref[1, p] * v_ref[p + 1]
        + c_ref[2, p] * turn(v, 1, 0)
        + c_ref[3, p] * turn(v, -1, 0)
        + c_ref[4, p] * turn(v, dup, 1)
        + c_ref[5, p] * turn(v, -dup, 1)
    )
    return v, source(p) - (c_ref[6, p] * v - summed)


def first_sweep(v_ref, source, c_ref, lo, hi, step=1):
    def plane(p):
        v_ref[p] = source(p) * c_ref[7, p]

    each(lo, hi, plane, step)


def sweep(v_ref, out_ref, source, c_ref, lo, hi, dup, step=1):
    def plane(p):
        v, rest = residual(v_ref, source, c_ref, p, dup)
        out_ref[p] = v + c_ref[7, p] * rest

    each(lo, hi, plane, step)


def restrict(pair, t_ref, slot, dup):
    lane = lanes_of(pair.shape)
    pair = pair + jnp.where(lane % (2 * dup) < dup, turn(pair, -dup, 1), turn(pair, dup, 1))
    count = pair.shape[0] // 2
    t_ref[slot, pl.ds(0, 2 * count), :] = pair
    even = t_ref[slot, pl.ds(0, count, stride=2), :]
    odd = t_ref[slot, pl.ds(1, count, stride=2), :]
    return (even + odd) * 0.125


def kernel(ngx, ngy, rhs, eps_in, scr_in, wts_in, chg_in, own_in, pot, atoms,
           eps, scr, wts, chg, own, sem_in,
           e0, fs, c0, va, vb, vc, t0,
           es1, e1, s1, f1, c1, ua, ub, uw, t1,
           g2es, g2f, e2, s2, f2, c2, xa, xb, u2, t2,
           grad, sb, rb,
           hello, sem_s0, sem_r0, sem_s1, sem_r1, sem_s2, sem_r2, sem_s3, sem_r3):
    cx, cy, nz = rhs.shape
    mx, my = cx // 2, cy // 2
    lx, ly = mx // 2, my // 2
    gx, gy = lax.axis_index("gx"), lax.axis_index("gy")
    total = ngx * ngy

    def peer(k):
        return lax.rem(gx + k // ngy, ngx), lax.rem(gy + k % ngy, ngy)

    def fill(ref, value):
        def plane(p):
            ref[p] = jnp.full(ref.shape[1:], value, F32)
        each(0, ref.shape[0], plane)

    loads = [pltpu.make_async_copy(a, b, sem_in.at[i]) for i, (a, b) in enumerate((
        (eps_in, eps), (scr_in, scr), (wts_in, wts), (chg_in, chg), (own_in, own)))]
    for load in loads:
        load.start()

    fill(e0, 0.0)

    def fill_pair(p):
        fs[p, 0] = jnp.zeros(e0.shape[1:], F32)
        fs[p, 1] = jnp.full(e0.shape[1:], 1.0, F32)
    each(0, e0.shape[0], fill_pair)
    fill(es1, 0.0)
    fill(f1, 0.0)
    fill(uw, 0.0)

    load_f = pltpu.make_async_copy(
        rhs, fs.at[pl.ds(HX, cx), 0, pl.ds(HY, cy), :], sem_in.at[5])
    load_f.start()

    def near_ok(dx, dy):
        return (gx + dx >= 0) & (gx + dx < ngx) & (gy + dy >= 0) & (gy + dy < ngy)

    def greet(sem):
        for dx, dy in DIRS:
            @pl.when(near_ok(dx, dy))
            def _(dx=dx, dy=dy):
                pl.semaphore_signal(
                    sem, inc=1, device_id={"gx": gx + dx, "gy": gy + dy}, device_id_type=MESH)

    def greeted(sem):
        wide = 3 - jnp.where(gx == 0, 1, 0) - jnp.where(gx == ngx - 1, 1, 0)
        high = 3 - jnp.where(gy == 0, 1, 0) - jnp.where(gy == ngy - 1, 1, 0)
        pl.semaphore_wait(sem, wide * high - 1)

    barrier = pltpu.get_barrier_semaphore()

    greet(barrier)
    loads[0].wait()
    loads[1].wait()

    def stage(p):
        e0[HX + p, pl.ds(HY, cy), :] = eps[p].astype(F32)
        fs[HX + p, 1, pl.ds(HY, cy), :] = scr[p].astype(F32)
    each(0, cx, stage, 2)
    load_f.wait()
    greeted(barrier)

    sent = []

    def drain(count=None):
        for ok, make in sent[:count]:
            @pl.when(ok)
            def _(make=make):
                make().wait_send()
        del sent[:count]

    def exchange(ref, base, own_x, halo_x, rows, sems, at, span):
        pending = []
        for number, (dx, dy) in enumerate(DIRS):
            limits = span(dx, dy)
            if limits is None:
                continue
            first, last = limits
            if dx == 0:
                src_x, dst_x, planes = halo_x, halo_x, own_x
            elif dx > 0:
                planes = last - first
                src_x, dst_x = halo_x + own_x - last, halo_x - last
            else:
                planes = last - first
                src_x, dst_x = halo_x + first, halo_x + own_x + first
            if dy == 0:
                src_y, dst_y, height = HY, HY, rows
            elif dy > 0:
                src_y, dst_y, height = rows, 0, HY
            else:
                src_y, dst_y, height = HY, HY + rows, HY
            target_ok = (gx + dx >= 0) & (gx + dx < ngx) & (gy + dy >= 0) & (gy + dy < ngy)
            source_ok = (gx - dx >= 0) & (gx - dx < ngx) & (gy - dy >= 0) & (gy - dy < ngy)

            def make(dx=dx, dy=dy, src_x=src_x, dst_x=dst_x, planes=planes,
                     src_y=src_y, dst_y=dst_y, height=height, number=number):
                fields = (slice(None),) * (len(ref.shape) - 3)
                return pltpu.make_async_remote_copy(
                    src_ref=ref.at[(pl.ds(src_x, planes), *fields, pl.ds(src_y, height))],
                    dst_ref=ref.at[(pl.ds(dst_x, planes), *fields, pl.ds(dst_y, height))],
                    send_sem=sems[0].at[at, number],
                    recv_sem=sems[1].at[at, number],
                    device_id={"gx": gx + dx, "gy": gy + dy},
                    device_id_type=MESH,
                )

            @pl.when(target_ok)
            def _(make=make):
                make().start()

            sent.append((target_ok, make))
            pending.append((dx, source_ok, make))

        def wait(along=None):
            for dx, ok, make in pending:
                if along is not None and (dx == 0) != (along == "y"):
                    continue

                @pl.when(ok)
                def _(make=make):
                    make().wait_recv()
        return wait

    def gather(ref, sems, at):
        def make(k):
            px, py = peer(k)
            spot = ref.at[gx, pl.ds(pl.multiple_of(gy * ly, ly), ly), :]
            return pltpu.make_async_remote_copy(
                src_ref=spot, dst_ref=spot,
                send_sem=sems[0].at[at, k], recv_sem=sems[1].at[at, k],
                device_id={"gx": px, "gy": py}, device_id_type=MESH,
            )

        def start(k, carry):
            make(k).start()
            return carry

        def finish(k, carry):
            make(k).wait_recv()
            return carry

        def release(k, carry):
            make(k).wait_send()
            return carry
        def for_peers(action):
            if total > 16:
                lax.fori_loop(1, total, action, 0)
            else:
                for k in range(1, total):
                    action(k, 0)

        for_peers(start)
        return (lambda: for_peers(finish)), (lambda: for_peers(release))

    rounds = max(ngx, ngy) - 2

    fine = (sem_s0, sem_r0)
    if rounds > 0:
        greet(hello.at[0])
    early_e = exchange(e0, 0, cx, HX, cy, fine, 0, lambda dx, dy: (0, 3))
    early_fs = exchange(fs, 0, cx, HX, cy, fine, 1, lambda dx, dy: (0, 2))

    def coarsen(i):
        pe = e0[HX + 2 * i, pl.ds(HY, cy), :] + e0[HX + 2 * i + 1, pl.ds(HY, cy), :]
        ps = fs[HX + 2 * i, 1, pl.ds(HY, cy), :] + fs[HX + 2 * i + 1, 1, pl.ds(HY, cy), :]
        me, ms = restrict(pe, t0, 0, 1), restrict(ps, t0, 1, 1)
        e1[mx + i, pl.ds(HY, my), :] = me
        s1[mx + i, pl.ds(HY, my), :] = ms
        es1[mx + i, pl.ds(HY, my), :] = jnp.where(lanes_of(me.shape) % 2 == 0, me, ms)
    for i in range(mx):
        coarsen(i)
    packed = []
    for ref in (e1, s1):
        for i in range(lx):
            pair = (ref[mx + 2 * i, pl.ds(HY, my), :] + ref[mx + 2 * i + 1, pl.ds(HY, my), :])
            packed.append(restrict(pair, t1, len(packed), 2))
    lane4 = lanes_of((ly, nz)) % 4
    g2es[gx, pl.ds(pl.multiple_of(gy * ly, ly), ly), :] = jnp.where(
        lane4 == 0, packed[0],
        jnp.where(lane4 == 1, packed[1], jnp.where(lane4 == 2, packed[2], packed[3])))

    mid = (sem_s1, sem_r1)
    wait_es1 = exchange(es1, 0, mx, mx, my, mid, 0, lambda dx, dy: (0, mx))
    low = (sem_s2, sem_r2)

    loads[3].wait()
    loads[4].wait()
    peers, atom_count = ngx, own.shape[2]
    capacity = 2 * atom_count // peers
    lane = lanes_of((atom_count, nz))
    square = lanes_of((atom_count, atom_count)) == rows_of((atom_count, atom_count))
    owner = jnp.sum(jnp.where(square, own[0], 0), axis=1, keepdims=True)
    hot = (owner == lane).astype(F32)
    before = (lanes_of((atom_count, atom_count)) < rows_of((atom_count, atom_count))).astype(F32)
    prior = jnp.dot(before, hot, preferred_element_type=F32)
    place = jnp.sum(prior * hot, axis=1, keepdims=True).astype(jnp.int32) + owner * capacity
    placing = (place == lane).astype(F32)
    charge = jnp.sum(jnp.where(square, chg[0], 0.0), axis=1, keepdims=True)

    def inside0(p, row):
        x = gx * cx + p - HX
        y = gy * cy + row - HY
        x_ok = jnp.where((x >= 0) & (x < ngx * cx), 1, 0)
        return (y >= 0) & (y < ngy * cy) & (row * 0 + x_ok > 0)

    def inside1(p, row):
        x = gx * mx + p - mx
        y = gy * my + row - HY
        x_ok = jnp.where((x >= 0) & (x < ngx * mx), 1, 0)
        return (y >= 0) & (y < ngy * my) & (row * 0 + x_ok > 0)

    rhs0 = lambda p: fs[p, 0]
    top = HX + cx
    for early in (early_e, early_fs):
        early("y")

    def begin(lo, hi, step):
        coefficients(e0, lambda p: fs[p, 1], c0, lo, hi, 1.0, 1, inside0, False, step)
        first_sweep(va, rhs0, c0, lo, hi, step)

    if rounds > 0:
        def spread_word(r, carry):
            greeted(hello.at[r])
            greet(hello.at[r + 1])
            return carry
        if rounds > 1:
            lax.fori_loop(0, rounds - 1, spread_word, 0)
    begin(HX + 1, top - 1, 2)
    sweep(va, vb, rhs0, c0, HX + 2, top - 2, 1, 2)
    if rounds > 0:
        greeted(hello.at[rounds - 1])
    wait_g2es, free_g2es = gather(g2es, low, 0)
    for early in (early_e, early_fs):
        early("x")
    begin(HX - 2, HX + 1, 3)
    begin(top - 1, top + 2, 3)
    sweep(va, vb, rhs0, c0, HX - 1, HX + 2, 1, 3)
    sweep(va, vb, rhs0, c0, top - 2, top + 1, 1, 3)

    def down(i):
        _, r0 = residual(vb, rhs0, c0, HX + 2 * i, 1)
        _, r1 = residual(vb, rhs0, c0, HX + 2 * i + 1, 1)
        f1[mx + i, pl.ds(HY, my), :] = restrict((r0 + r1)[HY:HY + cy], t0, i, 1)
    each(0, mx, down, mx)

    wait_f1 = exchange(f1, 0, mx, mx, my, mid, 1, lambda dx, dy: (0, 2 if dx and dy else 3))

    late_e = exchange(e0, 0, cx, HX, cy, fine, 3,
                      lambda dx, dy: None if dx == 0 else ((3, 4) if dy else (3, 5)))
    late_fs = exchange(fs, 0, cx, HX, cy, fine, 4,
                      lambda dx, dy: None if dx == 0 else ((2, 3) if dy else (2, 4)))

    wait_es1()

    def split(p):
        both = es1[p]
        even = lanes_of(both.shape) % 2 == 0
        e1[p] = jnp.where(even, both, turn(both, 1, 1))
        s1[p] = jnp.where(even, turn(both, -1, 1), both)
    each(0, 3 * mx, split, 4)
    src1 = lambda p: f1[p]
    coefficients(e1, lambda p: jnp.where(s1[p] > 0.0, s1[p], 1.0), c1, 1, 3 * mx - 1, 0.25, 2,
                 inside1, False, 2)
    wait_f1()
    first_sweep(ua, src1, c1, mx - 2, 2 * mx + 2, 4)
    sweep(ua, ub, src1, c1, mx - 1, 2 * mx + 1, 2, 3)
    parts = []
    for i in range(lx):
        _, r0 = residual(ub, src1, c1, mx + 2 * i, 2)
        _, r1 = residual(ub, src1, c1, mx + 2 * i + 1, 2)
        parts.append(restrict((r0 + r1)[HY:HY + my], t1, i, 2))
    g2f[gx, pl.ds(pl.multiple_of(gy * ly, ly), ly), :] = jnp.where(lane4 < 2, parts[0], parts[1])
    wait_g2f, free_g2f = gather(g2f, low, 1)
    earlier = len(sent)
    for i in range(mx):
        uw[mx + i, pl.ds(HY, my), :] = ub[mx + i, pl.ds(HY, my), :]
    wait_uw = exchange(uw, 0, mx, mx, my, mid, 2, lambda dx, dy: (0, mx))

    wait_g2es()
    rows_low = ngy * ly
    planes_low = ngx * lx
    for ref in (e2, xa, xb):
        ref[0] = jnp.zeros((rows_low, nz), F32)
        ref[planes_low + 1] = jnp.zeros((rows_low, nz), F32)
    quad = lanes_of((rows_low, nz)) % 4

    def spread(both, which):
        alone = jnp.where(quad == which, both, 0.0)
        twice = alone + turn(alone, 1 if which % 2 == 0 else -1, 1)
        return twice + turn(twice, 2 if which < 2 else -2, 1)

    def unpack(g):
        both = g2es[g]
        for i in range(lx):
            e2[1 + lx * g + i] = spread(both, i)
            s2[1 + lx * g + i] = spread(both, lx + i)
    each(0, ngx, unpack)
    coefficients(e2, lambda p: s2[p], c2, 1, planes_low + 1, 0.0625, 4, None, True, 2)

    late_e()
    late_fs()
    for lo, hi in ((HX - 4, HX - 2), (top + 2, top + 4)):
        begin(lo, hi, 2)
    sweep(va, vb, rhs0, c0, HX - 3, HX - 1, 1, 2)
    sweep(va, vb, rhs0, c0, top + 1, top + 3, 1, 2)
    fill(u2, 0.0)
    drain(earlier)

    free_g2es()
    wait_g2f()

    def source2(g):
        both = g2f[g]
        f2[1 + lx * g] = jnp.where(quad < 2, both, turn(both, 2, 1))
        f2[2 + lx * g] = jnp.where(quad < 2, turn(both, -2, 1), both)
    each(0, ngx, source2, 2)
    src2 = lambda p: f2[p]
    first_sweep(xa, src2, c2, 1, planes_low + 1, 4)
    here, there = xa, xb
    for _ in range(COARSE_SWEEPS - 1):
        sweep(here, there, src2, c2, 1, planes_low + 1, 4, 4)
        here, there = there, here
    for_u2 = here

    def keep(p):
        u2[2 + p, pl.ds(HY, rows_low), :] = for_u2[1 + p]
    each(0, planes_low, keep, 4)

    wait_uw()
    for i in range(3 * lx):
        near = u2[lx * gx + i, pl.ds(pl.multiple_of(gy * ly, ly), 3 * ly), :]
        near = near[ly // 2:ly // 2 + 2 * ly]
        t2[pl.ds(0, 2 * ly, stride=2), :] = near
        t2[pl.ds(1, 2 * ly, stride=2), :] = near
        child = t2[...]
        ua[2 * i] = uw[2 * i] + child
        ua[2 * i + 1] = uw[2 * i + 1] + child
    sweep(ua, ub, src1, c1, 1, 3 * mx - 1, 2, 2)
    sweep(ub, ua, src1, c1, 2, 3 * mx - 2, 2, 4)

    for c in range(mx - 2, 2 * mx + 2):
        near = ua[c][HY // 2:HY // 2 + (cy + 2 * HY) // 2]
        count = near.shape[0]
        t0[c - mx + 2, pl.ds(0, count, stride=2), :] = near
        t0[c - mx + 2, pl.ds(1, count, stride=2), :] = near
        child = t0[c - mx + 2]
        for p in (HX + 2 * (c - mx), HX + 2 * (c - mx) + 1):
            if HX - 3 <= p < top + 3:
                va[p] = vb[p] + child
    sweep(va, vc, rhs0, c0, HX - 2, top + 2, 1, 3)
    sweep(vc, va, rhs0, c0, HX - 1, top + 1, 1, 2)
    store = pltpu.make_async_copy(
        va.at[pl.ds(HX, cx), pl.ds(HY, cy), :], pot, sem_in.at[5])
    store.start()

    lane = lanes_of((cy // 8, 8, nz))
    row = rows_of((cy // 8, 8, nz))

    def swap(a):
        for bit in (1, 2, 4):
            r, g = (row // bit) % 2, (lane // (16 * bit)) % 2
            one = turn(turn(a, -bit, 1), 16 * bit, 2)
            other = one if bit == 4 else turn(turn(a, bit, 1), -16 * bit, 2)
            a = jnp.where(r == g, a, jnp.where(r == 0, one, other))
        return a

    def atoms_of(x, sums):
        p = HX + x
        v = va[p]
        lane_v = lanes_of(v.shape)
        up = jnp.where(lane_v == nz - 1, 0.0, turn(v, -1, 1))
        down_z = jnp.where(lane_v == 0, 0.0, turn(v, 1, 1))
        steps = ((va[p + 1] - va[p - 1]) * 0.5,
                 (turn(v, -1, 0) - turn(v, 1, 0)) * 0.5,
                 (up - down_z) * 0.5)
        tiles = [swap(g[HY:HY + cy].astype(jnp.bfloat16).astype(F32).reshape(cy // 8, 8, nz))
                 for g in steps]
        sums = list(sums)
        for q in range(cy // 8):
            at = pl.multiple_of(x * (cy * 16) + q * nz, nz)
            w = wts[0, 0, :, :, pl.ds(at, nz)].astype(F32)
            for k in range(3):
                sums[k] = sums[k] + w * tiles[k][q][:, None, :]
        return tuple(sums)

    blocks, slots = wts.shape[2], wts.shape[3]
    zero = jnp.zeros((blocks, slots, nz), F32)

    def atoms_of_four(i, carry):
        for j in range(4):
            carry = atoms_of(4 * i + j, carry)
        return carry

    loads[2].wait()
    sums = lax.fori_loop(0, cx // 4, atoms_of_four, (zero, zero, zero))
    row8 = rows_of((8, nz))
    result = jnp.zeros((8, nz), F32)
    for k in range(3):
        force = -charge * jnp.sum(sums[k].reshape(blocks * slots, nz), axis=1, keepdims=True)
        line = jnp.sum(force * placing, axis=0, keepdims=True)
        result = jnp.where(row8 == k, line, result)
    for t in range(peers):
        sb[t] = turn(result, -t * capacity, 1)

    def to_owner(o):
        target = lax.rem(gx + o, peers)
        return pltpu.make_async_remote_copy(
            src_ref=sb.at[target], dst_ref=rb.at[gx],
            send_sem=sem_s3.at[o], recv_sem=sem_r3.at[o],
            device_id={"gx": target, "gy": gy}, device_id_type=MESH)
    for o in range(1, peers):
        to_owner(o).start()
    rb[gx] = sb[gx]
    drain()
    free_g2f()
    for o in range(1, peers):
        to_owner(o).wait_recv()
    for t in range(peers):
        atoms[0, 0, t] = rb[t][:3, :capacity]
    for o in range(1, peers):
        to_owner(o).wait_send()
    store.wait()


def solution(mesh):
    ngx, ngy = mesh.shape["gx"], mesh.shape["gy"]

    def shards(right_side, dielectric, screening, weights, charges, owners):
        cx, cy, nz = right_side.shape
        capacity = 2 * owners.shape[2] // ngx
        vmem = lambda *shape: pltpu.VMEM(shape, F32)
        x0, y0 = cx + 2 * HX, cy + 2 * HY
        mx, my = cx // 2, cy // 2
        x1, y1 = 3 * mx, my + 2 * HY
        lx, ly = mx // 2, my // 2
        x2, y2 = ngx * lx, ngy * ly
        w0, w1, w2 = (x0, y0, nz), (x1, y1, nz), (x2 + 2, y2, nz)
        scratch = [
            pltpu.VMEM((cx, cy, nz), jnp.bfloat16), pltpu.VMEM((cx, cy, nz), jnp.bfloat16),
            pltpu.VMEM(weights.shape, jnp.bfloat16), vmem(*charges.shape),
            pltpu.VMEM(charges.shape, jnp.int32), pltpu.SemaphoreType.DMA((6,)),
            vmem(*w0), vmem(x0, 2, y0, nz), vmem(8, *w0), vmem(*w0), vmem(*w0), vmem(*w0),
            vmem(mx + 4, y0, nz),
            vmem(*w1), vmem(*w1), vmem(*w1), vmem(*w1), vmem(8, *w1), vmem(*w1), vmem(*w1),
            vmem(*w1), vmem(4, my, nz),
            vmem(ngx, y2, nz), vmem(ngx, y2, nz), vmem(*w2), vmem(*w2), vmem(*w2),
            vmem(8, *w2), vmem(*w2), vmem(*w2), vmem(x2 + 4, y2 + 2 * HY, nz), vmem(4 * ly, nz),
            vmem(8, nz), vmem(ngx, 8, nz), vmem(ngx, 8, nz),
            pltpu.SemaphoreType.REGULAR((max(ngx, ngy, 3) - 2,)),
            pltpu.SemaphoreType.DMA((6, 8)), pltpu.SemaphoreType.DMA((6, 8)),
            pltpu.SemaphoreType.DMA((3, 8)), pltpu.SemaphoreType.DMA((3, 8)),
            pltpu.SemaphoreType.DMA((2, ngx * ngy)), pltpu.SemaphoreType.DMA((2, ngx * ngy)),
            pltpu.SemaphoreType.DMA((ngx,)), pltpu.SemaphoreType.DMA((ngx,)),
        ]

        def body(*refs):
            kernel(ngx, ngy, *refs)

        return pl.pallas_call(
            body,
            out_shape=(
                jax.ShapeDtypeStruct((cx, cy, nz), F32),
                jax.ShapeDtypeStruct((1, 1, ngx, 3, capacity), F32),
            ),
            in_specs=[pl.BlockSpec(memory_space=pl.ANY)] * 6,
            out_specs=(pl.BlockSpec(memory_space=pl.ANY), pl.BlockSpec(memory_space=pltpu.VMEM)),
            scratch_shapes=scratch,
            compiler_params=pltpu.CompilerParams(
                collective_id=0, has_side_effects=True, vmem_limit_bytes=60 * 2**20
            ),
        )(right_side, dielectric, screening, weights, charges, owners.reshape(charges.shape))

    in_specs = (
        P(("rep", "gx"), "gy", None),
        P(("rep", "gx"), "gy", None),
        P(("rep", "gx"), "gy", None),
        P(("rep", "gx"), "gy", None, None, None),
        P(("rep", "gx"), "gy", None),
        P(("rep", "gx"), "gy", None, None),
    )
    out_specs = (P(("rep", "gx"), "gy", None), P(("rep", "gx"), "gy", None, None, None))
    return jax.shard_map(shards, mesh=mesh, in_specs=in_specs, out_specs=out_specs, check_vma=False)
```

```python
import jax
import jax.numpy as jnp
from jax import lax
from jax.experimental import pallas as pl
from jax.experimental.pallas import tpu as pltpu
from jax.sharding import PartitionSpec as P

POST_SWEEPS = 2
COARSE_SWEEPS = 6
OMEGA = 0.8
MESH = pl.DeviceIdType.MESH
F32 = jnp.float32
HX = 5
HY = 8
DIRS = ((1, 0), (-1, 0), (0, 1), (0, -1), (1, 1), (1, -1), (-1, 1), (-1, -1))


def turn(a, shift, axis):
    return pltpu.roll(a, shift % a.shape[axis], axis)


def each(lo, hi, body, step=1):
    count = hi - lo
    step = step if count % step == 0 else 1

    def group(i, carry):
        for j in range(step):
            body(lo + i * step + j)
        return carry

    lax.fori_loop(0, count // step, group, 0)


def lanes_of(shape):
    return lax.broadcasted_iota(jnp.int32, shape, len(shape) - 1)


def rows_of(shape):
    return lax.broadcasted_iota(jnp.int32, shape, len(shape) - 2)


def coefficients(e_ref, screen, c_ref, lo, hi, factor, dup, inside, closed, step=1):
    def plane(p):
        e = e_ref[p]
        lane = lanes_of(e.shape)
        row = rows_of(e.shape)
        low_z, high_z = lane < dup, lane >= e.shape[1] - dup
        near = [e_ref[p - 1], e_ref[p + 1], turn(e, 1, 0), turn(e, -1, 0)]
        if closed:
            low_y, high_y = row < 1, row >= e.shape[0] - 1
            near[2] = jnp.where(low_y, 0.0, near[2])
            near[3] = jnp.where(high_y, 0.0, near[3])
        near.append(jnp.where(low_z, 0.0, turn(e, dup, 1)))
        near.append(jnp.where(high_z, 0.0, turn(e, -dup, 1)))
        faces = [(0.5 * factor) * (e + other) for other in near]
        diagonal = faces[0] + faces[1] + faces[2] + faces[3] + faces[4] + faces[5] + screen(p)
        if closed:
            faces[2] = jnp.where(low_y, 0.0, faces[2])
            faces[3] = jnp.where(high_y, 0.0, faces[3])
        faces[4] = jnp.where(low_z, 0.0, faces[4])
        faces[5] = jnp.where(high_z, 0.0, faces[5])
        for k in range(6):
            c_ref[k, p] = faces[k]
        c_ref[6, p] = diagonal
        ratio = OMEGA / diagonal
        c_ref[7, p] = ratio if inside is None else jnp.where(inside(p, row), ratio, 0.0)

    each(lo, hi, plane, step)


def residual(v_ref, source, c_ref, p, dup):
    v = v_ref[p]
    summed = (
        c_ref[0, p] * v_ref[p - 1]
        + c_ref[1, p] * v_ref[p + 1]
        + c_ref[2, p] * turn(v, 1, 0)
        + c_ref[3, p] * turn(v, -1, 0)
        + c_ref[4, p] * turn(v, dup, 1)
        + c_ref[5, p] * turn(v, -dup, 1)
    )
    return v, source(p) - (c_ref[6, p] * v - summed)


def first_sweep(v_ref, source, c_ref, lo, hi, step=1):
    def plane(p):
        v_ref[p] = source(p) * c_ref[7, p]

    each(lo, hi, plane, step)


def sweep(v_ref, out_ref, source, c_ref, lo, hi, dup, step=1):
    def plane(p):
        v, rest = residual(v_ref, source, c_ref, p, dup)
        out_ref[p] = v + c_ref[7, p] * rest

    each(lo, hi, plane, step)


def restrict(pair, t_ref, slot, dup):
    lane = lanes_of(pair.shape)
    pair = pair + jnp.where(lane % (2 * dup) < dup, turn(pair, -dup, 1), turn(pair, dup, 1))
    count = pair.shape[0] // 2
    t_ref[slot, pl.ds(0, 2 * count), :] = pair
    even = t_ref[slot, pl.ds(0, count, stride=2), :]
    odd = t_ref[slot, pl.ds(1, count, stride=2), :]
    return (even + odd) * 0.125


def kernel(ngx, ngy, rhs, eps_in, scr_in, wts_in, chg_in, own_in, pot, atoms,
           eps, scr, wts, chg, own, sem_in,
           e0, fs, c0, va, vb, vc, t0,
           es1, e1, s1, f1, c1, ua, ub, uw, t1,
           g2es, g2f, e2, s2, f2, c2, xa, xb, u2, t2,
           grad, sb, rb,
           hello, sem_s0, sem_r0, sem_s1, sem_r1, sem_s2, sem_r2, sem_s3, sem_r3):
    cx, cy, nz = rhs.shape
    mx, my = cx // 2, cy // 2
    lx, ly = mx // 2, my // 2
    gx, gy = lax.axis_index("gx"), lax.axis_index("gy")
    total = ngx * ngy

    def peer(k):
        return lax.rem(gx + k // ngy, ngx), lax.rem(gy + k % ngy, ngy)

    def fill(ref, value):
        def plane(p):
            ref[p] = jnp.full(ref.shape[1:], value, F32)
        each(0, ref.shape[0], plane)

    loads = [pltpu.make_async_copy(a, b, sem_in.at[i]) for i, (a, b) in enumerate((
        (eps_in, eps), (scr_in, scr), (wts_in, wts), (chg_in, chg), (own_in, own)))]
    for load in loads:
        load.start()

    fill(e0, 0.0)

    def fill_pair(p):
        fs[p, 0] = jnp.zeros(e0.shape[1:], F32)
        fs[p, 1] = jnp.full(e0.shape[1:], 1.0, F32)
    each(0, e0.shape[0], fill_pair)
    fill(es1, 0.0)
    fill(f1, 0.0)
    fill(uw, 0.0)

    load_f = pltpu.make_async_copy(
        rhs, fs.at[pl.ds(HX, cx), 0, pl.ds(HY, cy), :], sem_in.at[5])
    load_f.start()

    def near_ok(dx, dy):
        return (gx + dx >= 0) & (gx + dx < ngx) & (gy + dy >= 0) & (gy + dy < ngy)

    def greet(sem):
        for dx, dy in DIRS:
            @pl.when(near_ok(dx, dy))
            def _(dx=dx, dy=dy):
                pl.semaphore_signal(
                    sem, inc=1, device_id={"gx": gx + dx, "gy": gy + dy}, device_id_type=MESH)

    def greeted(sem):
        wide = 3 - jnp.where(gx == 0, 1, 0) - jnp.where(gx == ngx - 1, 1, 0)
        high = 3 - jnp.where(gy == 0, 1, 0) - jnp.where(gy == ngy - 1, 1, 0)
        pl.semaphore_wait(sem, wide * high - 1)

    barrier = pltpu.get_barrier_semaphore()

    greet(barrier)
    loads[0].wait()
    loads[1].wait()

    def stage(p):
        e0[HX + p, pl.ds(HY, cy), :] = eps[p].astype(F32)
        fs[HX + p, 1, pl.ds(HY, cy), :] = scr[p].astype(F32)
    each(0, cx, stage, 2)
    load_f.wait()
    greeted(barrier)

    sent = []

    def drain(count=None):
        for ok, make in sent[:count]:
            @pl.when(ok)
            def _(make=make):
                make().wait_send()
        del sent[:count]

    def exchange(ref, base, own_x, halo_x, rows, sems, at, span):
        pending = []
        for number, (dx, dy) in enumerate(DIRS):
            limits = span(dx, dy)
            if limits is None:
                continue
            first, last = limits
            if dx == 0:
                src_x, dst_x, planes = halo_x, halo_x, own_x
            elif dx > 0:
                planes = last - first
                src_x, dst_x = halo_x + own_x - last, halo_x - last
            else:
                planes = last - first
                src_x, dst_x = halo_x + first, halo_x + own_x + first
            if dy == 0:
                src_y, dst_y, height = HY, HY, rows
            elif dy > 0:
                src_y, dst_y, height = rows, 0, HY
            else:
                src_y, dst_y, height = HY, HY + rows, HY
            target_ok = (gx + dx >= 0) & (gx + dx < ngx) & (gy + dy >= 0) & (gy + dy < ngy)
            source_ok = (gx - dx >= 0) & (gx - dx < ngx) & (gy - dy >= 0) & (gy - dy < ngy)

            def make(dx=dx, dy=dy, src_x=src_x, dst_x=dst_x, planes=planes,
                     src_y=src_y, dst_y=dst_y, height=height, number=number):
                fields = (slice(None),) * (len(ref.shape) - 3)
                return pltpu.make_async_remote_copy(
                    src_ref=ref.at[(pl.ds(src_x, planes), *fields, pl.ds(src_y, height))],
                    dst_ref=ref.at[(pl.ds(dst_x, planes), *fields, pl.ds(dst_y, height))],
                    send_sem=sems[0].at[at, number],
                    recv_sem=sems[1].at[at, number],
                    device_id={"gx": gx + dx, "gy": gy + dy},
                    device_id_type=MESH,
                )

            @pl.when(target_ok)
            def _(make=make):
                make().start()

            sent.append((target_ok, make))
            pending.append((dx, source_ok, make))

        def wait(along=None):
            for dx, ok, make in pending:
                if along is not None and (dx == 0) != (along == "y"):
                    continue

                @pl.when(ok)
                def _(make=make):
                    make().wait_recv()
        return wait

    def gather(ref, sems, at):
        def make(k):
            px, py = peer(k)
            spot = ref.at[gx, pl.ds(pl.multiple_of(gy * ly, ly), ly), :]
            return pltpu.make_async_remote_copy(
                src_ref=spot, dst_ref=spot,
                send_sem=sems[0].at[at, k], recv_sem=sems[1].at[at, k],
                device_id={"gx": px, "gy": py}, device_id_type=MESH,
            )

        def start(k, carry):
            make(k).start()
            return carry

        def finish(k, carry):
            make(k).wait_recv()
            return carry

        def release(k, carry):
            make(k).wait_send()
            return carry
        def for_peers(action):
            if total > 16:
                lax.fori_loop(1, total, action, 0)
            else:
                for k in range(1, total):
                    action(k, 0)

        for_peers(start)
        return (lambda: for_peers(finish)), (lambda: for_peers(release))

    rounds = max(ngx, ngy) - 2

    fine = (sem_s0, sem_r0)
    if rounds > 0:
        greet(hello.at[0])
    early_e = exchange(e0, 0, cx, HX, cy, fine, 0, lambda dx, dy: (0, 3))
    early_fs = exchange(fs, 0, cx, HX, cy, fine, 1, lambda dx, dy: (0, 2))

    def coarsen(i):
        pe = e0[HX + 2 * i, pl.ds(HY, cy), :] + e0[HX + 2 * i + 1, pl.ds(HY, cy), :]
        ps = fs[HX + 2 * i, 1, pl.ds(HY, cy), :] + fs[HX + 2 * i + 1, 1, pl.ds(HY, cy), :]
        me, ms = restrict(pe, t0, 0, 1), restrict(ps, t0, 1, 1)
        e1[mx + i, pl.ds(HY, my), :] = me
        s1[mx + i, pl.ds(HY, my), :] = ms
        es1[mx + i, pl.ds(HY, my), :] = jnp.where(lanes_of(me.shape) % 2 == 0, me, ms)
    for i in range(mx):
        coarsen(i)
    packed = []
    for ref in (e1, s1):
        for i in range(lx):
            pair = (ref[mx + 2 * i, pl.ds(HY, my), :] + ref[mx + 2 * i + 1, pl.ds(HY, my), :])
            packed.append(restrict(pair, t1, len(packed), 2))
    lane4 = lanes_of((ly, nz)) % 4
    g2es[gx, pl.ds(pl.multiple_of(gy * ly, ly), ly), :] = jnp.where(
        lane4 == 0, packed[0],
        jnp.where(lane4 == 1, packed[1], jnp.where(lane4 == 2, packed[2], packed[3])))

    mid = (sem_s1, sem_r1)
    wait_es1 = exchange(es1, 0, mx, mx, my, mid, 0, lambda dx, dy: (0, mx))
    low = (sem_s2, sem_r2)

    loads[3].wait()
    loads[4].wait()
    peers, atom_count = ngx, own.shape[2]
    capacity = 2 * atom_count // peers
    lane = lanes_of((atom_count, nz))
    square = lanes_of((atom_count, atom_count)) == rows_of((atom_count, atom_count))
    owner = jnp.sum(jnp.where(square, own[0], 0), axis=1, keepdims=True)
    hot = (owner == lane).astype(F32)
    before = (lanes_of((atom_count, atom_count)) < rows_of((atom_count, atom_count))).astype(F32)
    prior = jnp.dot(before, hot, preferred_element_type=F32)
    place = jnp.sum(prior * hot, axis=1, keepdims=True).astype(jnp.int32) + owner * capacity
    placing = (place == lane).astype(F32)
    charge = jnp.sum(jnp.where(square, chg[0], 0.0), axis=1, keepdims=True)

    def inside0(p, row):
        x = gx * cx + p - HX
        y = gy * cy + row - HY
        x_ok = jnp.where((x >= 0) & (x < ngx * cx), 1, 0)
        return (y >= 0) & (y < ngy * cy) & (row * 0 + x_ok > 0)

    def inside1(p, row):
        x = gx * mx + p - mx
        y = gy * my + row - HY
        x_ok = jnp.where((x >= 0) & (x < ngx * mx), 1, 0)
        return (y >= 0) & (y < ngy * my) & (row * 0 + x_ok > 0)

    rhs0 = lambda p: fs[p, 0]
    top = HX + cx
    for early in (early_e, early_fs):
        early("y")

    def begin(lo, hi, step):
        coefficients(e0, lambda p: fs[p, 1], c0, lo, hi, 1.0, 1, inside0, False, step)
        first_sweep(va, rhs0, c0, lo, hi, step)

    if rounds > 0:
        def spread_word(r, carry):
            greeted(hello.at[r])
            greet(hello.at[r + 1])
            return carry
        if rounds > 1:
            lax.fori_loop(0, rounds - 1, spread_word, 0)
    begin(HX + 1, top - 1, 2)
    sweep(va, vb, rhs0, c0, HX + 2, top - 2, 1, 2)
    if rounds > 0:
        greeted(hello.at[rounds - 1])
    wait_g2es, free_g2es = gather(g2es, low, 0)
    for early in (early_e, early_fs):
        early("x")
    begin(HX - 2, HX + 1, 3)
    begin(top - 1, top + 2, 3)
    sweep(va, vb, rhs0, c0, HX - 1, HX + 2, 1, 3)
    sweep(va, vb, rhs0, c0, top - 2, top + 1, 1, 3)

    def down(i):
        _, r0 = residual(vb, rhs0, c0, HX + 2 * i, 1)
        _, r1 = residual(vb, rhs0, c0, HX + 2 * i + 1, 1)
        f1[mx + i, pl.ds(HY, my), :] = restrict((r0 + r1)[HY:HY + cy], t0, i, 1)
    each(0, mx, down, mx)

    wait_f1 = exchange(f1, 0, mx, mx, my, mid, 1, lambda dx, dy: (0, 2 if dx and dy else 3))

    late_e = exchange(e0, 0, cx, HX, cy, fine, 3,
                      lambda dx, dy: None if dx == 0 else ((3, 4) if dy else (3, 5)))
    late_fs = exchange(fs, 0, cx, HX, cy, fine, 4,
                      lambda dx, dy: None if dx == 0 else ((2, 3) if dy else (2, 4)))

    wait_es1()

    def split(p):
        both = es1[p]
        even = lanes_of(both.shape) % 2 == 0
        e1[p] = jnp.where(even, both, turn(both, 1, 1))
        s1[p] = jnp.where(even, turn(both, -1, 1), both)
    each(0, 3 * mx, split, 4)
    src1 = lambda p: f1[p]
    coefficients(e1, lambda p: jnp.where(s1[p] > 0.0, s1[p], 1.0), c1, 1, 3 * mx - 1, 0.25, 2,
                 inside1, False, 5)
    wait_f1()
    first_sweep(ua, src1, c1, mx - 2, 2 * mx + 2, 4)
    sweep(ua, ub, src1, c1, mx - 1, 2 * mx + 1, 2, 6)
    parts = []
    for i in range(lx):
        _, r0 = residual(ub, src1, c1, mx + 2 * i, 2)
        _, r1 = residual(ub, src1, c1, mx + 2 * i + 1, 2)
        parts.append(restrict((r0 + r1)[HY:HY + my], t1, i, 2))
    g2f[gx, pl.ds(pl.multiple_of(gy * ly, ly), ly), :] = jnp.where(lane4 < 2, parts[0], parts[1])
    wait_g2f, free_g2f = gather(g2f, low, 1)
    earlier = len(sent)
    for i in range(mx):
        uw[mx + i, pl.ds(HY, my), :] = ub[mx + i, pl.ds(HY, my), :]
    wait_uw = exchange(uw, 0, mx, mx, my, mid, 2, lambda dx, dy: (0, mx))

    wait_g2es()
    rows_low = ngy * ly
    planes_low = ngx * lx
    for ref in (e2, xa, xb):
        ref[0] = jnp.zeros((rows_low, nz), F32)
        ref[planes_low + 1] = jnp.zeros((rows_low, nz), F32)
    quad = lanes_of((rows_low, nz)) % 4

    def spread(both, which):
        alone = jnp.where(quad == which, both, 0.0)
        twice = alone + turn(alone, 1 if which % 2 == 0 else -1, 1)
        return twice + turn(twice, 2 if which < 2 else -2, 1)

    def unpack(g):
        both = g2es[g]
        for i in range(lx):
            e2[1 + lx * g + i] = spread(both, i)
            s2[1 + lx * g + i] = spread(both, lx + i)
    each(0, ngx, unpack)
    coefficients(e2, lambda p: s2[p], c2, 1, planes_low + 1, 0.0625, 4, None, True, 4)

    late_e()
    late_fs()
    for lo, hi in ((HX - 4, HX - 2), (top + 2, top + 4)):
        begin(lo, hi, 2)
    sweep(va, vb, rhs0, c0, HX - 3, HX - 1, 1, 2)
    sweep(va, vb, rhs0, c0, top + 1, top + 3, 1, 2)
    fill(u2, 0.0)
    drain(earlier)

    free_g2es()
    wait_g2f()

    def source2(g):
        both = g2f[g]
        f2[1 + lx * g] = jnp.where(quad < 2, both, turn(both, 2, 1))
        f2[2 + lx * g] = jnp.where(quad < 2, turn(both, -2, 1), both)
    each(0, ngx, source2, 2)
    src2 = lambda p: f2[p]
    first_sweep(xa, src2, c2, 1, planes_low + 1, 4)
    here, there = xa, xb
    for _ in range(COARSE_SWEEPS - 1):
        sweep(here, there, src2, c2, 1, planes_low + 1, 4, 8)
        here, there = there, here
    for_u2 = here

    def keep(p):
        u2[2 + p, pl.ds(HY, rows_low), :] = for_u2[1 + p]
    each(0, planes_low, keep, 4)

    wait_uw()
    for i in range(3 * lx):
        near = u2[lx * gx + i, pl.ds(pl.multiple_of(gy * ly, ly), 3 * ly), :]
        near = near[ly // 2:ly // 2 + 2 * ly]
        t2[pl.ds(0, 2 * ly, stride=2), :] = near
        t2[pl.ds(1, 2 * ly, stride=2), :] = near
        child = t2[...]
        ua[2 * i] = uw[2 * i] + child
        ua[2 * i + 1] = uw[2 * i + 1] + child
    sweep(ua, ub, src1, c1, 1, 3 * mx - 1, 2, 5)
    sweep(ub, ua, src1, c1, 2, 3 * mx - 2, 2, 8)

    for c in range(mx - 2, 2 * mx + 2):
        near = ua[c][HY // 2:HY // 2 + (cy + 2 * HY) // 2]
        count = near.shape[0]
        t0[c - mx + 2, pl.ds(0, count, stride=2), :] = near
        t0[c - mx + 2, pl.ds(1, count, stride=2), :] = near
        child = t0[c - mx + 2]
        for p in (HX + 2 * (c - mx), HX + 2 * (c - mx) + 1):
            if HX - 3 <= p < top + 3:
                va[p] = vb[p] + child
    sweep(va, vc, rhs0, c0, HX - 2, top + 2, 1, 6)
    sweep(vc, va, rhs0, c0, HX - 1, top + 1, 1, 5)
    store = pltpu.make_async_copy(
        va.at[pl.ds(HX, cx), pl.ds(HY, cy), :], pot, sem_in.at[5])
    store.start()

    lane = lanes_of((cy // 8, 8, nz))
    row = rows_of((cy // 8, 8, nz))

    def swap(a):
        for bit in (1, 2, 4):
            r, g = (row // bit) % 2, (lane // (16 * bit)) % 2
            one = turn(turn(a, -bit, 1), 16 * bit, 2)
            other = one if bit == 4 else turn(turn(a, bit, 1), -16 * bit, 2)
            a = jnp.where(r == g, a, jnp.where(r == 0, one, other))
        return a

    def atoms_of(x, sums):
        p = HX + x
        v = va[p]
        lane_v = lanes_of(v.shape)
        up = jnp.where(lane_v == nz - 1, 0.0, turn(v, -1, 1))
        down_z = jnp.where(lane_v == 0, 0.0, turn(v, 1, 1))
        steps = ((va[p + 1] - va[p - 1]) * 0.5,
                 (turn(v, -1, 0) - turn(v, 1, 0)) * 0.5,
                 (up - down_z) * 0.5)
        tiles = [swap(g[HY:HY + cy].astype(jnp.bfloat16).astype(F32).reshape(cy // 8, 8, nz))
                 for g in steps]
        sums = list(sums)
        for q in range(cy // 8):
            at = pl.multiple_of(x * (cy * 16) + q * nz, nz)
            w = wts[0, 0, :, :, pl.ds(at, nz)].astype(F32)
            for k in range(3):
                sums[k] = sums[k] + w * tiles[k][q][:, None, :]
        return tuple(sums)

    blocks, slots = wts.shape[2], wts.shape[3]
    zero = jnp.zeros((blocks, slots, nz), F32)

    def atoms_of_four(i, carry):
        for j in range(4):
            carry = atoms_of(4 * i + j, carry)
        return carry

    loads[2].wait()
    sums = lax.fori_loop(0, cx // 4, atoms_of_four, (zero, zero, zero))
    row8 = rows_of((8, nz))
    result = jnp.zeros((8, nz), F32)
    for k in range(3):
        force = -charge * jnp.sum(sums[k].reshape(blocks * slots, nz), axis=1, keepdims=True)
        line = jnp.sum(force * placing, axis=0, keepdims=True)
        result = jnp.where(row8 == k, line, result)
    for t in range(peers):
        sb[t] = turn(result, -t * capacity, 1)

    def to_owner(o):
        target = lax.rem(gx + o, peers)
        return pltpu.make_async_remote_copy(
            src_ref=sb.at[target], dst_ref=rb.at[gx],
            send_sem=sem_s3.at[o], recv_sem=sem_r3.at[o],
            device_id={"gx": target, "gy": gy}, device_id_type=MESH)
    for o in range(1, peers):
        to_owner(o).start()
    rb[gx] = sb[gx]
    drain()
    free_g2f()
    for o in range(1, peers):
        to_owner(o).wait_recv()
    for t in range(peers):
        atoms[0, 0, t] = rb[t][:3, :capacity]
    for o in range(1, peers):
        to_owner(o).wait_send()
    store.wait()


def solution(mesh):
    ngx, ngy = mesh.shape["gx"], mesh.shape["gy"]

    def shards(right_side, dielectric, screening, weights, charges, owners):
        cx, cy, nz = right_side.shape
        capacity = 2 * owners.shape[2] // ngx
        vmem = lambda *shape: pltpu.VMEM(shape, F32)
        x0, y0 = cx + 2 * HX, cy + 2 * HY
        mx, my = cx // 2, cy // 2
        x1, y1 = 3 * mx, my + 2 * HY
        lx, ly = mx // 2, my // 2
        x2, y2 = ngx * lx, ngy * ly
        w0, w1, w2 = (x0, y0, nz), (x1, y1, nz), (x2 + 2, y2, nz)
        scratch = [
            pltpu.VMEM((cx, cy, nz), jnp.bfloat16), pltpu.VMEM((cx, cy, nz), jnp.bfloat16),
            pltpu.VMEM(weights.shape, jnp.bfloat16), vmem(*charges.shape),
            pltpu.VMEM(charges.shape, jnp.int32), pltpu.SemaphoreType.DMA((6,)),
            vmem(*w0), vmem(x0, 2, y0, nz), vmem(8, *w0), vmem(*w0), vmem(*w0), vmem(*w0),
            vmem(mx + 4, y0, nz),
            vmem(*w1), vmem(*w1), vmem(*w1), vmem(*w1), vmem(8, *w1), vmem(*w1), vmem(*w1),
            vmem(*w1), vmem(4, my, nz),
            vmem(ngx, y2, nz), vmem(ngx, y2, nz), vmem(*w2), vmem(*w2), vmem(*w2),
            vmem(8, *w2), vmem(*w2), vmem(*w2), vmem(x2 + 4, y2 + 2 * HY, nz), vmem(4 * ly, nz),
            vmem(8, nz), vmem(ngx, 8, nz), vmem(ngx, 8, nz),
            pltpu.SemaphoreType.REGULAR((max(ngx, ngy, 3) - 2,)),
            pltpu.SemaphoreType.DMA((6, 8)), pltpu.SemaphoreType.DMA((6, 8)),
            pltpu.SemaphoreType.DMA((3, 8)), pltpu.SemaphoreType.DMA((3, 8)),
            pltpu.SemaphoreType.DMA((2, ngx * ngy)), pltpu.SemaphoreType.DMA((2, ngx * ngy)),
            pltpu.SemaphoreType.DMA((ngx,)), pltpu.SemaphoreType.DMA((ngx,)),
        ]

        def body(*refs):
            kernel(ngx, ngy, *refs)

        return pl.pallas_call(
            body,
            out_shape=(
                jax.ShapeDtypeStruct((cx, cy, nz), F32),
                jax.ShapeDtypeStruct((1, 1, ngx, 3, capacity), F32),
            ),
            in_specs=[pl.BlockSpec(memory_space=pl.ANY)] * 6,
            out_specs=(pl.BlockSpec(memory_space=pl.ANY), pl.BlockSpec(memory_space=pltpu.VMEM)),
            scratch_shapes=scratch,
            compiler_params=pltpu.CompilerParams(
                collective_id=0, has_side_effects=True, vmem_limit_bytes=60 * 2**20
            ),
        )(right_side, dielectric, screening, weights, charges, owners.reshape(charges.shape))

    in_specs = (
        P(("rep", "gx"), "gy", None),
        P(("rep", "gx"), "gy", None),
        P(("rep", "gx"), "gy", None),
        P(("rep", "gx"), "gy", None, None, None),
        P(("rep", "gx"), "gy", None),
        P(("rep", "gx"), "gy", None, None),
    )
    out_specs = (P(("rep", "gx"), "gy", None), P(("rep", "gx"), "gy", None, None, None))
    return jax.shard_map(shards, mesh=mesh, in_specs=in_specs, out_specs=out_specs, check_vma=False)
```
